512 devices in a mesh: blk: 512 (over x, y, z, core).
Axes of the slice: x: 4, y: 4, z: 16, core: 2. Of those that a mesh axis runs over, the one named last changes fastest.
Arguments:
- embeddings: float32 [262144, 768], P('blk'), may hold values from -2 to 2
- labels: int32 [262144], P('blk'), may hold values from 0 to 255
Outputs:
- scores: float32 [262144, 256], P('blk')
The draws below stay inside these ranges and needn't reach their ends.
All inputs are finite; a program needn't handle non-finite values.
Results may differ from the reference program's by a relative error of at most 0.00077.
Values sent between devices are 32-bit elements; how exact they have to be, the bound alone decides.
No kernel may reach another device: no remote copies, remote signals or barrier semaphores. Data moves between devices by JAX's collectives and lax.ppermute only.
A program may use at most 64 MiB of HBM per device.

```python
import math
import jax
import jax.numpy as jnp
from jax import lax

ROWS = 512
DIM = 768
CLUSTERS = 256
STEPS = 6
TOTAL = 262144
N_BLK = 512


latent_dims = 8


def cluster_plan(key):
    label_key, other_key = jax.random.split(key, 2)
    assigned = jax.random.randint(label_key, (TOTAL,), 0, CLUSTERS, dtype=jnp.int32)
    home_cluster = jax.random.randint(other_key, (TOTAL,), 0, CLUSTERS, dtype=jnp.int32)
    return (assigned, home_cluster)


def draw_labels(key, part):
    assigned, home_cluster = cluster_plan(key)
    return assigned


def draw_embeddings(key, part):
    assigned, home_cluster = cluster_plan(key)
    key = jax.random.fold_in(key, 11)
    center_key, jitter_key, freq_key, phase_key, column_key, offset_key = jax.random.split(key, 6)
    centers = jax.random.normal(center_key, (CLUSTERS, latent_dims), jnp.float32)
    jitter = 0.15 * jax.random.normal(jitter_key, (TOTAL, latent_dims), jnp.float32)
    column_top = 10.0
    squared_scale = 1.5
    offset_size = 0.0
    latent = jnp.take(centers, home_cluster, axis=0) + jitter
    frequencies = jax.random.normal(freq_key, (latent_dims, DIM), jnp.float32)
    phases = jax.random.uniform(phase_key, (1, DIM), jnp.float32, 0.0, 2.0 * math.pi)
    for latent_axis in range(latent_dims):
        phases = phases + latent[:, latent_axis:latent_axis + 1] * frequencies[latent_axis:latent_axis + 1, :]
    amplitude = jnp.exp(jax.random.uniform(column_key, (1, DIM), jnp.float32, 0.0, math.log(column_top)))
    mean_square = (column_top * column_top - 1.0) / (2.0 * math.log(column_top))
    factor = math.sqrt(2.0 * squared_scale / mean_square) / jnp.sqrt(DIM * 1.0)
    shared = jax.random.uniform(offset_key, (1, DIM), jnp.float32, -1.7320508, 1.7320508)
    values = factor * amplitude * jnp.cos(phases) + offset_size / jnp.sqrt(DIM * 1.0) * shared
    return values.astype(jnp.float32)


def setup_inputs(seed: int = 0) -> dict:
    splits = jax.random.split(jax.random.key(seed), 3)
    return {
        "embeddings": draw_embeddings(jax.random.fold_in(splits[2], 71), 0),
        "labels": draw_labels(jax.random.fold_in(splits[2], 71), 0),
    }


def reference(embeddings, labels):
    blocks = embeddings.reshape(N_BLK, ROWS, DIM)
    row_norms = jnp.sum(blocks * blocks, axis=2)
    owned = labels.reshape(N_BLK, ROWS)
    onehot = (owned[:, :, None] == jnp.arange(CLUSTERS, dtype=jnp.int32)[None, None, :]).astype(jnp.float32)
    scores = jnp.zeros((N_BLK, ROWS, CLUSTERS), jnp.float32)
    for offset in range(STEPS + 1):
        other = jnp.roll(blocks, offset, axis=0)
        other_norms = jnp.roll(row_norms, offset, axis=0)
        other_hot = jnp.roll(onehot, offset, axis=0)
        inner = jnp.einsum("bid,bjd->bij", blocks, other, precision=lax.Precision.HIGHEST)
        kernel = jnp.exp(-(row_norms[:, :, None] + other_norms[:, None, :] - 2.0 * inner))
        kernel = kernel.astype(jnp.bfloat16).astype(jnp.float32)
        scores = scores + jnp.einsum("bij,bjc->bic", kernel, other_hot)
        if offset > 0:
            mirrored = jnp.einsum("bij,bic->bjc", kernel, onehot)
            scores = scores + jnp.roll(mirrored, -offset, axis=0)
    return scores.reshape(N_BLK * ROWS, CLUSTERS)
```

```python
import jax
import jax.numpy as jnp
from jax import lax
from jax.experimental import pallas as pl
from jax.experimental.pallas import tpu as pltpu
from jax.sharding import PartitionSpec as P

CLUSTERS = 256
TOP = 8


def even_odd(n, even, odd):
    return [(i, (i + (even if i % 2 == 0 else odd)) % n) for i in range(n)]


def pull(value):
    n = lax.axis_size("blk")
    return lax.ppermute(value, "blk", even_odd(n, -2, 2))


def push(value):
    n = lax.axis_size("blk")
    return lax.ppermute(value, "blk", even_odd(n, 2, -2))


def swap(value):
    n = lax.axis_size("blk")
    return lax.ppermute(value, "blk", even_odd(n, 1, -1))


def hot(message_ref, rows):
    cluster = lax.broadcasted_iota(jnp.int32, (CLUSTERS, rows), 0)
    same = cluster == message_ref[0:1, :rows].astype(jnp.int32)
    return jnp.where(same, 1.0, 0.0).astype(jnp.bfloat16)


def kernel_tile(left, right):
    left_norms = jnp.sum(left * left, axis=1, keepdims=True)
    right_norms = jnp.sum(right * right, axis=1, keepdims=True)
    right_norms = jnp.transpose(jnp.broadcast_to(right_norms, (right.shape[0], 128)))[0:1, :]
    inner = lax.dot_general(
        left,
        right,
        (((1,), (1,)), ((), ())),
        precision=lax.Precision.HIGHEST,
        preferred_element_type=jnp.float32,
    )
    return jnp.exp(-(left_norms + right_norms - 2.0 * inner)).astype(jnp.bfloat16)


def left_sums(right_hot, kernel):
    return lax.dot_general(
        right_hot, kernel, (((1,), (1,)), ((), ())), preferred_element_type=jnp.float32
    )


def right_sums(left_hot, kernel):
    return jnp.dot(left_hot, kernel, preferred_element_type=jnp.float32)


def self_body(own_ref, own_out):
    own = own_ref[TOP:, :]
    rows = own.shape[0]
    own_out[...] = left_sums(hot(own_ref, rows), kernel_tile(own, own))


def pair_body(left_ref, right_ref, left_in, right_in, left_out, right_out):
    left, right = left_ref[TOP:, :], right_ref[TOP:, :]
    rows = left.shape[0]
    kernel = kernel_tile(left, right)
    left_out[...] = left_in[...] + left_sums(hot(right_ref, rows), kernel)
    right_out[...] = right_in[...] + right_sums(hot(left_ref, rows), kernel)


def halves(left, left_hot, first_ref, second_ref, total, right_out):
    half = second_ref.shape[0]
    right_hot = hot(first_ref, 2 * half)
    for right, span in (
        (first_ref[TOP:, :], slice(0, half)),
        (second_ref[...], slice(half, 2 * half)),
    ):
        kernel = kernel_tile(left, right)
        total += left_sums(right_hot[:, span], kernel)
        right_out[:, span] += right_sums(left_hot, kernel)
    return total


def visitor_body(
    own_ref, b2_ref, first_ref, second_ref, own_in, for_2_in, own_out, for_2_out, for_y_out
):
    rows = own_ref.shape[0] - TOP
    for_y_out[...] = jnp.zeros_like(for_y_out)
    own_out[...] = halves(
        own_ref[TOP:, :], hot(own_ref, rows), first_ref, second_ref, own_in[...], for_y_out
    )
    for_2_out[...] = halves(
        b2_ref[TOP:, :], hot(b2_ref, rows), first_ref, second_ref, for_2_in[...], for_y_out
    )


def late_body(
    even_ref, bm2_ref, b4_ref, first_ref, second_ref, for_m2_in, for_y_in,
    for_m2_out, for_4_out, for_y_out,
):
    even = even_ref[0] == 1
    bm2, b4 = bm2_ref[TOP:, :], b4_ref[TOP:, :]
    rows = bm2.shape[0]
    kernel = kernel_tile(bm2, b4)
    bm2_hot, b4_hot = hot(bm2_ref, rows), hot(b4_ref, rows)
    for_m2_out[...] = for_m2_in[...] + left_sums(b4_hot, kernel)
    for_4_out[...] = right_sums(bm2_hot, kernel)
    for_y_out[...] = for_y_in[...]
    far = halves(
        jnp.where(even, bm2, b4),
        jnp.where(even, bm2_hot, b4_hot),
        first_ref,
        second_ref,
        jnp.zeros_like(for_y_out),
        for_y_out,
    )
    for_m2_out[...] += jnp.where(even, far, 0.0)
    for_4_out[...] += jnp.where(even, 0.0, far)


def call(body, outs, rows, *args):
    shape = jax.ShapeDtypeStruct((CLUSTERS, rows), jnp.float32)
    vmem = pl.BlockSpec(memory_space=pltpu.VMEM)
    smem = pl.BlockSpec(memory_space=pltpu.SMEM)
    return pl.pallas_call(
        body,
        out_shape=[shape] * outs,
        in_specs=[smem if a.ndim == 1 else vmem for a in args],
        out_specs=[vmem] * outs,
        compiler_params=pltpu.CompilerParams(vmem_limit_bytes=32 * 2**20),
        cost_estimate=pl.CostEstimate(flops=1000, bytes_accessed=1000, transcendentals=0),
    )(*args)


def on_device(embeddings, labels):
    rows, dim = embeddings.shape
    cut = TOP + rows // 2
    is_even = lax.axis_index("blk") % 2 == 0
    zero = jnp.zeros((CLUSTERS, rows), jnp.float32)
    top = jnp.pad(labels.astype(jnp.float32)[None, :], ((0, TOP - 1), (0, dim - rows)))
    own = jnp.concatenate([top, embeddings], axis=0)

    b2 = pull(own)
    (score,) = call(self_body, 1, rows, own)
    later_own, score = lax.optimization_barrier((own, score))
    bm2 = push(later_own)
    b4 = pull(b2)

    score, for_2 = call(pair_body, 2, rows, own, b2, score, zero)
    bm2, score, for_2 = lax.optimization_barrier((bm2, score, for_2))

    first = swap(jnp.where(is_even, b2[:cut], bm2[:cut]))
    second = swap(jnp.where(is_even, b2[cut:], bm2[cut:]))
    for_m2, for_2 = call(pair_body, 2, rows, bm2, b2, zero, for_2)

    first, second, for_2, for_m2 = lax.optimization_barrier((first, second, for_2, for_m2))
    score, for_2, for_y = call(visitor_body, 3, rows, own, b2, first, second, score, for_2)

    b4, score, for_2, for_m2, for_y = lax.optimization_barrier((b4, score, for_2, for_m2, for_y))
    even = is_even.astype(jnp.int32)[None]
    for_m2, for_4, for_y = call(
        late_body, 3, rows, even, bm2, b4, first, second, for_m2, for_y
    )
    back_4 = push(for_4)
    back_y = swap(for_y)
    m2_back = pull(for_m2 + jnp.where(is_even, 0.0, back_y))
    back_4, back_y, for_2 = lax.optimization_barrier((back_4, back_y, for_2))
    back_2 = push(for_2 + jnp.where(is_even, back_y, 0.0) + back_4)
    return (score + m2_back + back_2).T


def solution(mesh):
    placed = (P("blk", None), P("blk"))
    return jax.shard_map(
        on_device, mesh=mesh, in_specs=placed, out_specs=P("blk", None), check_vma=False
    )
```

```python
import jax
import jax.numpy as jnp
from jax import lax
from jax.experimental import pallas as pl
from jax.experimental.pallas import tpu as pltpu
from jax.sharding import PartitionSpec as P

CLUSTERS = 256
TOP = 8
END = 8


def even_odd(n, even, odd):
    return [(i, (i + (even if i % 2 == 0 else odd)) % n) for i in range(n)]


def pull(value):
    n = lax.axis_size("blk")
    return lax.ppermute(value, "blk", even_odd(n, -2, 2))


def push(value):
    n = lax.axis_size("blk")
    return lax.ppermute(value, "blk", even_odd(n, 2, -2))


def swap(value):
    n = lax.axis_size("blk")
    return lax.ppermute(value, "blk", even_odd(n, 1, -1))


def give(value, core):
    n = lax.axis_size("blk")
    return lax.ppermute(value, "blk", [(i, i ^ 1) for i in range(core, n, 2)])


def one_hot(labels):
    cluster = lax.broadcasted_iota(jnp.int32, (CLUSTERS, labels.shape[1]), 0)
    return jnp.where(cluster == labels.astype(jnp.int32), 1.0, 0.0).astype(jnp.bfloat16)


def unpack(message):
    rows = (message.shape[0] - TOP) // 128 * 128
    return message[TOP : TOP + rows, :], one_hot(message[0:1, :rows])


def pack_body(embeddings_ref, labels_ref, message_ref, held, done):
    rows = embeddings_ref.shape[0]
    copy = pltpu.make_async_copy(embeddings_ref, message_ref.at[pl.ds(TOP, rows)], done.at[0])
    copy.start()
    labels = pltpu.make_async_copy(labels_ref, held, done.at[1])
    labels.start()
    message_ref[:TOP, :] = jnp.zeros((TOP, message_ref.shape[1]), jnp.float32)
    message_ref[TOP + rows :, :] = jnp.zeros((END, message_ref.shape[1]), jnp.float32)
    labels.wait()
    message_ref[0:1, :rows] = held[...].astype(jnp.float32)
    copy.wait()


def pack(embeddings, labels):
    rows, dim = embeddings.shape
    return pl.pallas_call(
        pack_body,
        out_shape=pltpu.VMEM((TOP + rows + END, dim), jnp.float32),
        in_specs=[pl.BlockSpec(memory_space=pltpu.HBM)] * 2,
        out_specs=pl.BlockSpec(memory_space=pltpu.VMEM),
        scratch_shapes=[pltpu.VMEM((1, rows), jnp.int32), pltpu.SemaphoreType.DMA((2,))],
        compiler_params=pltpu.CompilerParams(vmem_limit_bytes=16 * 2**20),
    )(
        pltpu.with_memory_space_constraint(embeddings, pltpu.HBM),
        pltpu.with_memory_space_constraint(labels[None, :], pltpu.HBM),
    )


def kernel_tile(left, right):
    left_norms = jnp.sum(left * left, axis=1, keepdims=True)
    right_norms = jnp.sum(right * right, axis=1, keepdims=True)
    right_norms = jnp.transpose(jnp.broadcast_to(right_norms, (right.shape[0], 128)))[0:1, :]
    inner = lax.dot_general(
        left,
        right,
        (((1,), (1,)), ((), ())),
        precision=lax.Precision.HIGHEST,
        preferred_element_type=jnp.float32,
    )
    return jnp.exp(-(left_norms + right_norms - 2.0 * inner)).astype(jnp.bfloat16)


def left_sums(right_hot, kernel):
    return lax.dot_general(
        right_hot, kernel, (((1,), (1,)), ((), ())), preferred_element_type=jnp.float32
    )


def right_sums(left_hot, kernel):
    return jnp.dot(left_hot, kernel, preferred_element_type=jnp.float32)


def self_body(own_ref, own_in, own_out):
    own, own_hot = unpack(own_ref)
    own_out[...] = own_in[...] + left_sums(own_hot, kernel_tile(own, own))


def pair_body(left_ref, right_ref, left_in, right_in, left_out, right_out):
    left, left_hot = unpack(left_ref)
    right, right_hot = unpack(right_ref)
    kernel = kernel_tile(left, right)
    left_out[...] = left_in[...] + left_sums(right_hot, kernel)
    right_out[...] = right_in[...] + right_sums(left_hot, kernel)


def visitor(even_y_ref, odd_y_ref):
    return unpack(even_y_ref[...] + odd_y_ref[...])


def visitor_body(
    even_ref, own_ref, bm2_ref, b2_ref, even_y_ref, odd_y_ref, own_in, for_m2_in, for_2_in,
    own_out, for_m2_out, for_2_out, for_y_out,
):
    y, y_hot = visitor(even_y_ref, odd_y_ref)
    own, own_hot = unpack(own_ref)
    kernel = kernel_tile(own, y)
    own_out[...] = own_in[...] + left_sums(y_hot, kernel)
    for_y_out[...] = right_sums(own_hot, kernel)
    b2, b2_hot = unpack(b2_ref)
    kernel = kernel_tile(b2, y)
    for_2_out[...] = for_2_in[...] + left_sums(y_hot, kernel)
    for_y_out[...] += right_sums(b2_hot, kernel)
    for_m2_out[...] = for_m2_in[...]

    @pl.when(even_ref[0] == 1)
    def _():
        bm2, bm2_hot = unpack(bm2_ref)
        kernel = kernel_tile(bm2, y)
        for_m2_out[...] += left_sums(y_hot, kernel)
        for_y_out[...] += right_sums(bm2_hot, kernel)


def late_body(
    even_ref, bm2_ref, b4_ref, even_y_ref, odd_y_ref, for_m2_in, for_y_in,
    for_m2_out, for_4_out, for_y_out,
):
    b4, b4_hot = unpack(b4_ref)
    bm2, bm2_hot = unpack(bm2_ref)
    kernel = kernel_tile(bm2, b4)
    for_m2_out[...] = for_m2_in[...] + left_sums(b4_hot, kernel)
    for_4_out[...] = right_sums(bm2_hot, kernel)
    for_y_out[...] = for_y_in[...]

    @pl.when(even_ref[0] == 0)
    def _():
        y, y_hot = visitor(even_y_ref, odd_y_ref)
        kernel = kernel_tile(b4, y)
        for_4_out[...] += left_sums(y_hot, kernel)
        for_y_out[...] += right_sums(b4_hot, kernel)


def call(body, outs, *args, flops=1000):
    rows = args[-1].shape[1]
    vmem = pl.BlockSpec(memory_space=pltpu.VMEM)
    smem = pl.BlockSpec(memory_space=pltpu.SMEM)
    return pl.pallas_call(
        body,
        out_shape=[pltpu.VMEM((CLUSTERS, rows), jnp.float32)] * outs,
        in_specs=[smem if a.ndim == 1 else vmem for a in args],
        out_specs=[vmem] * outs,
        compiler_params=pltpu.CompilerParams(vmem_limit_bytes=16 * 2**20),
        cost_estimate=pl.CostEstimate(flops=flops, bytes_accessed=1000, transcendentals=0),
    )(*(a if a.ndim == 1 else pltpu.with_memory_space_constraint(a, pltpu.VMEM) for a in args))


def on_device(embeddings, labels):
    rows = embeddings.shape[0]
    is_even = lax.axis_index("blk") % 2 == 0
    even = is_even.astype(jnp.int32)[None]
    zero = jnp.zeros((CLUSTERS, rows), jnp.float32)
    own = pack(embeddings, labels)

    b2 = pull(own)
    bm2 = push(own[: TOP + rows])
    (score,) = call(self_body, 1, own, zero)
    b2, score = lax.optimization_barrier((b2, score))
    b4 = pull(b2)

    score, for_2 = call(pair_body, 2, own, b2, score, zero)
    b2, score, for_2 = lax.optimization_barrier((b2, score, for_2))
    even_y = give(b2[: TOP + rows], 0)
    bm2, score, for_2 = lax.optimization_barrier((bm2, score, for_2))
    odd_y = give(bm2, 1)
    for_m2, for_2 = call(pair_body, 2, bm2, b2, zero, for_2)

    even_y, odd_y, for_2, for_m2 = lax.optimization_barrier((even_y, odd_y, for_2, for_m2))
    score, for_m2, for_2, for_y = call(
        visitor_body, 4, even, own, bm2, b2, even_y, odd_y, score, for_m2, for_2
    )
    back_m2 = give(for_y, 0)

    b4, score, for_2, for_m2, for_y = lax.optimization_barrier((b4, score, for_2, for_m2, for_y))
    for_m2, for_4, for_y = call(
        late_body, 3, even, bm2, b4, even_y, odd_y, for_m2, for_y, flops=12 * rows * rows * 768
    )
    back_4 = push(for_4)
    home_m2 = pull(for_m2 + back_m2)
    back_2 = give(for_y, 1)
    home_2 = push(for_2 + back_2 + back_4)
    return (score + home_m2 + home_2).T


def solution(mesh):
    placed = (P("blk", None), P("blk"))
    return jax.shard_map(
        on_device, mesh=mesh, in_specs=placed, out_specs=P("blk", None), check_vma=False
    )
```

```python
import jax
import jax.numpy as jnp
from jax import lax
from jax.experimental import pallas as pl
from jax.experimental.pallas import tpu as pltpu
from jax.sharding import PartitionSpec as P

CLUSTERS = 256
TOP = 8


def even_odd(n, even, odd):
    return [(i, (i + (even if i % 2 == 0 else odd)) % n) for i in range(n)]


def pull(value):
    n = lax.axis_size("blk")
    return lax.ppermute(value, "blk", even_odd(n, -2, 2))


def push(value):
    n = lax.axis_size("blk")
    return lax.ppermute(value, "blk", even_odd(n, 2, -2))


def swap(value):
    n = lax.axis_size("blk")
    return lax.ppermute(value, "blk", even_odd(n, 1, -1))


def give(value, core):
    n = lax.axis_size("blk")
    return lax.ppermute(value, "blk", [(i, i ^ 1) for i in range(core, n, 2)])


def one_hot(labels):
    cluster = lax.broadcasted_iota(jnp.int32, (CLUSTERS, labels.shape[1]), 0)
    return jnp.where(cluster == labels.astype(jnp.int32), 1.0, 0.0).astype(jnp.bfloat16)


def unpack(message):
    rows = message.shape[0] - TOP
    return message[TOP:, :], one_hot(message[0:1, :rows])


def pack_body(embeddings_ref, labels_ref, message_ref, held, done):
    rows = embeddings_ref.shape[0]
    copy = pltpu.make_async_copy(embeddings_ref, message_ref.at[pl.ds(TOP, rows)], done.at[0])
    copy.start()
    labels = pltpu.make_async_copy(labels_ref, held, done.at[1])
    labels.start()
    message_ref[:TOP, :] = jnp.zeros((TOP, message_ref.shape[1]), jnp.float32)
    labels.wait()
    message_ref[0:1, :rows] = held[...].astype(jnp.float32)
    copy.wait()


def pack(embeddings, labels):
    rows, dim = embeddings.shape
    return pl.pallas_call(
        pack_body,
        out_shape=pltpu.VMEM((TOP + rows, dim), jnp.float32),
        in_specs=[pl.BlockSpec(memory_space=pltpu.HBM)] * 2,
        out_specs=pl.BlockSpec(memory_space=pltpu.VMEM),
        scratch_shapes=[pltpu.VMEM((1, rows), jnp.int32), pltpu.SemaphoreType.DMA((2,))],
        compiler_params=pltpu.CompilerParams(vmem_limit_bytes=16 * 2**20),
    )(
        pltpu.with_memory_space_constraint(embeddings, pltpu.HBM),
        pltpu.with_memory_space_constraint(labels[None, :], pltpu.HBM),
    )


def kernel_tile(left, right):
    left_norms = jnp.sum(left * left, axis=1, keepdims=True)
    right_norms = jnp.sum(right * right, axis=1, keepdims=True)
    right_norms = jnp.transpose(jnp.broadcast_to(right_norms, (right.shape[0], 128)))[0:1, :]
    inner = lax.dot_general(
        left,
        right,
        (((1,), (1,)), ((), ())),
        precision=lax.Precision.HIGHEST,
        preferred_element_type=jnp.float32,
    )
    return jnp.exp(-(left_norms + right_norms - 2.0 * inner)).astype(jnp.bfloat16)


def left_sums(right_hot, kernel):
    return lax.dot_general(
        right_hot, kernel, (((1,), (1,)), ((), ())), preferred_element_type=jnp.float32
    )


def right_sums(left_hot, kernel):
    return jnp.dot(left_hot, kernel, preferred_element_type=jnp.float32)


def self_body(own_ref, own_out):
    own, own_hot = unpack(own_ref)
    own_out[...] = left_sums(own_hot, kernel_tile(own, own))


def pair_body(left_ref, right_ref, left_out, right_out):
    left, left_hot = unpack(left_ref)
    right, right_hot = unpack(right_ref)
    kernel = kernel_tile(left, right)
    left_out[...] = left_sums(right_hot, kernel)
    right_out[...] = right_sums(left_hot, kernel)


def visitor_body(
    even_ref, own_ref, bm2_ref, b2_ref, y_top_ref, y_end_ref,
    own_out, for_m2_out, for_2_out, for_y_out,
):
    y, y_hot = unpack(jnp.concatenate([y_top_ref[...], y_end_ref[...]], axis=0))
    own, own_hot = unpack(own_ref)
    kernel = kernel_tile(own, y)
    own_out[...] = left_sums(y_hot, kernel)
    for_y_out[...] = right_sums(own_hot, kernel)
    b2, b2_hot = unpack(b2_ref)
    kernel = kernel_tile(b2, y)
    for_2_out[...] = left_sums(y_hot, kernel)
    for_y_out[...] += right_sums(b2_hot, kernel)
    for_m2_out[...] = jnp.zeros_like(for_m2_out)

    @pl.when(even_ref[0] == 1)
    def _():
        bm2, bm2_hot = unpack(bm2_ref)
        kernel = kernel_tile(bm2, y)
        for_m2_out[...] = left_sums(y_hot, kernel)
        for_y_out[...] += right_sums(bm2_hot, kernel)


def late_body(
    even_ref, bm2_ref, b4_ref, y_top_ref, y_end_ref, for_y_in, for_m2_out, for_4_out, for_y_out
):
    b4, b4_hot = unpack(b4_ref)
    bm2, bm2_hot = unpack(bm2_ref)
    kernel = kernel_tile(bm2, b4)
    for_m2_out[...] = left_sums(b4_hot, kernel)
    for_4_out[...] = right_sums(bm2_hot, kernel)
    for_y_out[...] = for_y_in[...]

    @pl.when(even_ref[0] == 0)
    def _():
        y, y_hot = unpack(jnp.concatenate([y_top_ref[...], y_end_ref[...]], axis=0))
        kernel = kernel_tile(b4, y)
        for_4_out[...] += left_sums(y_hot, kernel)
        for_y_out[...] += right_sums(b4_hot, kernel)


def call(body, outs, rows, *args, moved=1000):
    vmem = pl.BlockSpec(memory_space=pltpu.VMEM)
    smem = pl.BlockSpec(memory_space=pltpu.SMEM)
    return pl.pallas_call(
        body,
        out_shape=[pltpu.VMEM((CLUSTERS, rows), jnp.float32)] * outs,
        in_specs=[smem if a.ndim == 1 else vmem for a in args],
        out_specs=[vmem] * outs,
        compiler_params=pltpu.CompilerParams(vmem_limit_bytes=16 * 2**20),
        cost_estimate=pl.CostEstimate(flops=1000, bytes_accessed=moved, transcendentals=0),
    )(*(a if a.ndim == 1 else pltpu.with_memory_space_constraint(a, pltpu.VMEM) for a in args))


def on_device(embeddings, labels):
    rows = embeddings.shape[0]
    is_even = lax.axis_index("blk") % 2 == 0
    even = is_even.astype(jnp.int32)[None]
    own = pack(embeddings, labels)

    b2 = pull(own)
    bm2 = push(own)
    (own_0,) = call(self_body, 1, rows, own, moved=4 * own.size)
    b2, own_0 = lax.optimization_barrier((b2, own_0))
    b4 = pull(b2)

    b2, bm2 = lax.optimization_barrier((b2, bm2))
    own_2, for_2 = call(pair_body, 2, rows, own, b2, moved=1000)
    cut = TOP + rows // 2
    y = (
        swap(jnp.where(is_even, b2[:cut], bm2[:cut])),
        swap(jnp.where(is_even, b2[cut:], bm2[cut:])),
    )
    for_m2, for_2_m2 = call(pair_body, 2, rows, bm2, b2)

    y, own_2, for_2, for_m2, for_2_m2 = lax.optimization_barrier(
        (y, own_2, for_2, for_m2, for_2_m2)
    )
    own_y, for_m2_y, for_2_y, for_y = call(visitor_body, 4, rows, even, own, bm2, b2, *y)
    back_m2 = give(for_y, 0)

    b4, own_y, for_m2_y, for_2_y, for_y = lax.optimization_barrier(
        (b4, own_y, for_m2_y, for_2_y, for_y)
    )
    for_m2_4, for_4, for_y = call(
        late_body, 3, rows, even, bm2, b4, *y, for_y, moved=16 * own.size
    )
    back_4 = push(for_4)
    home_m2 = pull(for_m2 + for_m2_y + for_m2_4 + back_m2)
    back_2 = give(for_y, 1)
    back_4, back_2, for_2 = lax.optimization_barrier((back_4, back_2, for_2 + for_2_m2 + for_2_y))
    home_2 = push(for_2 + back_2 + back_4)
    return (own_0 + own_2 + own_y + home_m2 + home_2).T


def solution(mesh):
    placed = (P("blk", None), P("blk"))
    return jax.shard_map(
        on_device, mesh=mesh, in_specs=placed, out_specs=P("blk", None), check_vma=False
    )
```

```python
import jax
import jax.numpy as jnp
from jax import lax
from jax.experimental import pallas as pl
from jax.experimental.pallas import tpu as pltpu
from jax.sharding import PartitionSpec as P

CLUSTERS = 256
TOP = 8


def even_odd(n, even, odd):
    return [(i, (i + (even if i % 2 == 0 else odd)) % n) for i in range(n)]


def pull(value):
    n = lax.axis_size("blk")
    return lax.ppermute(value, "blk", even_odd(n, -2, 2))


def push(value):
    n = lax.axis_size("blk")
    return lax.ppermute(value, "blk", even_odd(n, 2, -2))


def swap(value):
    n = lax.axis_size("blk")
    return lax.ppermute(value, "blk", even_odd(n, 1, -1))


def give(value, core):
    n = lax.axis_size("blk")
    return lax.ppermute(value, "blk", [(i, i ^ 1) for i in range(core, n, 2)])


def one_hot(labels):
    cluster = lax.broadcasted_iota(jnp.int32, (CLUSTERS, labels.shape[1]), 0)
    return jnp.where(cluster == labels.astype(jnp.int32), 1.0, 0.0).astype(jnp.bfloat16)


def unpack(message):
    rows = message.shape[0] - TOP
    return message[TOP:, :], one_hot(message[0:1, :rows])


def pack_body(embeddings_ref, labels_ref, message_ref, held, done):
    rows = embeddings_ref.shape[0]
    copy = pltpu.make_async_copy(embeddings_ref, message_ref.at[pl.ds(TOP, rows)], done.at[0])
    copy.start()
    labels = pltpu.make_async_copy(labels_ref, held, done.at[1])
    labels.start()
    message_ref[:TOP, :] = jnp.zeros((TOP, message_ref.shape[1]), jnp.float32)
    labels.wait()
    message_ref[0:1, :rows] = held[...].astype(jnp.float32)
    copy.wait()


def pack(embeddings, labels):
    rows, dim = embeddings.shape
    return pl.pallas_call(
        pack_body,
        out_shape=pltpu.VMEM((TOP + rows, dim), jnp.float32),
        in_specs=[pl.BlockSpec(memory_space=pltpu.HBM)] * 2,
        out_specs=pl.BlockSpec(memory_space=pltpu.VMEM),
        scratch_shapes=[pltpu.VMEM((1, rows), jnp.int32), pltpu.SemaphoreType.DMA((2,))],
        compiler_params=pltpu.CompilerParams(vmem_limit_bytes=16 * 2**20),
    )(
        pltpu.with_memory_space_constraint(embeddings, pltpu.HBM),
        pltpu.with_memory_space_constraint(labels[None, :], pltpu.HBM),
    )


def kernel_tile(left, right):
    left_norms = jnp.sum(left * left, axis=1, keepdims=True)
    right_norms = jnp.sum(right * right, axis=1, keepdims=True)
    right_norms = jnp.transpose(jnp.broadcast_to(right_norms, (right.shape[0], 128)))[0:1, :]
    inner = lax.dot_general(
        left,
        right,
        (((1,), (1,)), ((), ())),
        precision=lax.Precision.HIGHEST,
        preferred_element_type=jnp.float32,
    )
    return jnp.exp(-(left_norms + right_norms - 2.0 * inner)).astype(jnp.bfloat16)


def left_sums(right_hot, kernel):
    return lax.dot_general(
        right_hot, kernel, (((1,), (1,)), ((), ())), preferred_element_type=jnp.float32
    )


def right_sums(left_hot, kernel):
    return jnp.dot(left_hot, kernel, preferred_element_type=jnp.float32)


def self_body(own_ref, own_out):
    own, own_hot = unpack(own_ref)
    own_out[...] = left_sums(own_hot, kernel_tile(own, own))


def pair_body(left_ref, right_ref, left_out, right_out):
    left, left_hot = unpack(left_ref)
    right, right_hot = unpack(right_ref)
    kernel = kernel_tile(left, right)
    left_out[...] = left_sums(right_hot, kernel)
    right_out[...] = right_sums(left_hot, kernel)


def visitor_body(
    even_ref, own_ref, bm2_ref, b2_ref, y_top_ref, y_end_ref,
    own_out, for_m2_out, for_2_out, for_y_out,
):
    y, y_hot = unpack(jnp.concatenate([y_top_ref[...], y_end_ref[...]], axis=0))
    own, own_hot = unpack(own_ref)
    kernel = kernel_tile(own, y)
    own_out[...] = left_sums(y_hot, kernel)
    for_y_out[...] = right_sums(own_hot, kernel)
    b2, b2_hot = unpack(b2_ref)
    kernel = kernel_tile(b2, y)
    for_2_out[...] = left_sums(y_hot, kernel)
    for_y_out[...] += right_sums(b2_hot, kernel)
    for_m2_out[...] = jnp.zeros_like(for_m2_out)

    @pl.when(even_ref[0] == 1)
    def _():
        bm2, bm2_hot = unpack(bm2_ref)
        kernel = kernel_tile(bm2, y)
        for_m2_out[...] = left_sums(y_hot, kernel)
        for_y_out[...] += right_sums(bm2_hot, kernel)


def late_body(
    even_ref, bm2_ref, b4_ref, y_top_ref, y_end_ref, for_y_in, for_m2_out, for_4_out, for_y_out
):
    b4, b4_hot = unpack(b4_ref)
    bm2, bm2_hot = unpack(bm2_ref)
    kernel = kernel_tile(bm2, b4)
    for_m2_out[...] = left_sums(b4_hot, kernel)
    for_4_out[...] = right_sums(bm2_hot, kernel)
    for_y_out[...] = for_y_in[...]

    @pl.when(even_ref[0] == 0)
    def _():
        y, y_hot = unpack(jnp.concatenate([y_top_ref[...], y_end_ref[...]], axis=0))
        kernel = kernel_tile(b4, y)
        for_4_out[...] += left_sums(y_hot, kernel)
        for_y_out[...] += right_sums(b4_hot, kernel)


def choose_body(even_ref, b2_ref, bm2_ref, top_out, end_out):
    cut = top_out.shape[0]

    @pl.when(even_ref[0] == 1)
    def _():
        top_out[...] = b2_ref[:cut, :]
        end_out[...] = b2_ref[cut:, :]

    @pl.when(even_ref[0] == 0)
    def _():
        top_out[...] = bm2_ref[:cut, :]
        end_out[...] = bm2_ref[cut:, :]


def call(body, shapes, *args, moved=1000):
    vmem = pl.BlockSpec(memory_space=pltpu.VMEM)
    smem = pl.BlockSpec(memory_space=pltpu.SMEM)
    return pl.pallas_call(
        body,
        out_shape=[pltpu.VMEM(shape, jnp.float32) for shape in shapes],
        in_specs=[smem if a.ndim == 1 else vmem for a in args],
        out_specs=[vmem] * len(shapes),
        compiler_params=pltpu.CompilerParams(vmem_limit_bytes=16 * 2**20),
        cost_estimate=pl.CostEstimate(flops=1000, bytes_accessed=moved, transcendentals=0),
    )(*(a if a.ndim == 1 else pltpu.with_memory_space_constraint(a, pltpu.VMEM) for a in args))


def on_device(embeddings, labels):
    rows, dim = embeddings.shape
    cut = TOP + rows // 2
    sums = (CLUSTERS, rows)
    even = swap((lax.axis_index("blk") % 2).astype(jnp.int32)[None])
    own = pack(embeddings, labels)
    own, even = lax.optimization_barrier((own, even))

    b2 = pull(own)
    bm2 = push(own)
    (own_0,) = call(self_body, [sums], own, moved=4 * own.size)
    b2, own_0 = lax.optimization_barrier((b2, own_0))
    b4 = pull(b2)

    b2, bm2 = lax.optimization_barrier((b2, bm2))
    y_top, y_end = call(
        choose_body, [(cut, dim), (rows + TOP - cut, dim)], even, b2, bm2, moved=8 * own.size
    )
    y = swap(y_top), swap(y_end)
    own_2, for_2 = call(pair_body, [sums] * 2, own, b2, moved=8 * own.size)
    for_m2, for_2_m2 = call(pair_body, [sums] * 2, bm2, b2, moved=8 * own.size)

    y, own_2, for_2, for_m2, for_2_m2 = lax.optimization_barrier(
        (y, own_2, for_2, for_m2, for_2_m2)
    )
    own_y, for_m2_y, for_2_y, for_y = call(
        visitor_body, [sums] * 4, even, own, bm2, b2, *y, moved=8 * own.size
    )
    back_m2 = give(for_y, 0)

    b4, own_y, for_m2_y, for_2_y, for_y = lax.optimization_barrier(
        (b4, own_y, for_m2_y, for_2_y, for_y)
    )
    for_m2_4, for_4, for_y = call(
        late_body, [sums] * 3, even, bm2, b4, *y, for_y, moved=16 * own.size
    )
    back_4 = push(for_4)
    home_m2 = pull(for_m2 + for_m2_y + for_m2_4 + back_m2)
    back_2 = give(for_y, 1)
    back_4, back_2, for_2 = lax.optimization_barrier((back_4, back_2, for_2 + for_2_m2 + for_2_y))
    home_2 = push(for_2 + back_2 + back_4)
    return (own_0 + own_2 + own_y + home_m2 + home_2).T


def solution(mesh):
    placed = (P("blk", None), P("blk"))
    return jax.shard_map(
        on_device, mesh=mesh, in_specs=placed, out_specs=P("blk", None), check_vma=False
    )
```

```python
import jax
import jax.numpy as jnp
from jax import lax
from jax.experimental import pallas as pl
from jax.experimental.pallas import tpu as pltpu
from jax.sharding import PartitionSpec as P

CLUSTERS = 256
TOP = 8


def even_odd(n, even, odd):
    return [(i, (i + (even if i % 2 == 0 else odd)) % n) for i in range(n)]


def pull(value):
    n = lax.axis_size("blk")
    return lax.ppermute(value, "blk", even_odd(n, -2, 2))


def push(value, chips=1):
    n = lax.axis_size("blk")
    return lax.ppermute(value, "blk", even_odd(n, 2 * chips, -2 * chips))


def swap(value):
    n = lax.axis_size("blk")
    return lax.ppermute(value, "blk", even_odd(n, 1, -1))


def give(value, core):
    n = lax.axis_size("blk")
    return lax.ppermute(value, "blk", [(i, i ^ 1) for i in range(core, n, 2)])


def one_hot(labels):
    cluster = lax.broadcasted_iota(jnp.int32, (CLUSTERS, labels.shape[1]), 0)
    return jnp.where(cluster == labels.astype(jnp.int32), 1.0, 0.0).astype(jnp.bfloat16)


def unpack(message):
    rows = message.shape[0] - TOP
    return message[TOP:, :], one_hot(message[0:1, :rows])


def pack_body(embeddings_ref, labels_ref, message_ref, held, done):
    rows = embeddings_ref.shape[0]
    copy = pltpu.make_async_copy(embeddings_ref, message_ref.at[pl.ds(TOP, rows)], done.at[0])
    copy.start()
    labels = pltpu.make_async_copy(labels_ref, held, done.at[1])
    labels.start()
    message_ref[:TOP, :] = jnp.zeros((TOP, message_ref.shape[1]), jnp.float32)
    labels.wait()
    message_ref[0:1, :rows] = held[...].astype(jnp.float32)
    copy.wait()


def pack(embeddings, labels):
    rows, dim = embeddings.shape
    return pl.pallas_call(
        pack_body,
        out_shape=pltpu.VMEM((TOP + rows, dim), jnp.float32),
        in_specs=[pl.BlockSpec(memory_space=pltpu.HBM)] * 2,
        out_specs=pl.BlockSpec(memory_space=pltpu.VMEM),
        scratch_shapes=[pltpu.VMEM((1, rows), jnp.int32), pltpu.SemaphoreType.DMA((2,))],
        compiler_params=pltpu.CompilerParams(vmem_limit_bytes=16 * 2**20),
    )(
        pltpu.with_memory_space_constraint(embeddings, pltpu.HBM),
        pltpu.with_memory_space_constraint(labels[None, :], pltpu.HBM),
    )


def kernel_tile(left, right):
    left_norms = jnp.sum(left * left, axis=1, keepdims=True)
    right_norms = jnp.sum(right * right, axis=1, keepdims=True)
    right_norms = jnp.transpose(jnp.broadcast_to(right_norms, (right.shape[0], 128)))[0:1, :]
    inner = lax.dot_general(
        left,
        right,
        (((1,), (1,)), ((), ())),
        precision=lax.Precision.HIGHEST,
        preferred_element_type=jnp.float32,
    )
    return jnp.exp(-(left_norms + right_norms - 2.0 * inner)).astype(jnp.bfloat16)


def left_sums(right_hot, kernel):
    return lax.dot_general(
        right_hot, kernel, (((1,), (1,)), ((), ())), preferred_element_type=jnp.float32
    )


def right_sums(left_hot, kernel):
    return jnp.dot(left_hot, kernel, preferred_element_type=jnp.float32)


def self_body(own_ref, own_out):
    own, own_hot = unpack(own_ref)
    own_out[...] = left_sums(own_hot, kernel_tile(own, own))


def pair_body(left_ref, right_ref, left_out, right_out):
    left, left_hot = unpack(left_ref)
    right, right_hot = unpack(right_ref)
    kernel = kernel_tile(left, right)
    left_out[...] = left_sums(right_hot, kernel)
    right_out[...] = right_sums(left_hot, kernel)


def visitor_body(
    even_ref, own_ref, bm2_ref, b2_ref, y_top_ref, y_end_ref,
    own_out, for_m2_out, for_2_out, for_y_out,
):
    y, y_hot = unpack(jnp.concatenate([y_top_ref[...], y_end_ref[...]], axis=0))
    own, own_hot = unpack(own_ref)
    kernel = kernel_tile(own, y)
    own_out[...] = left_sums(y_hot, kernel)
    for_y_out[...] = right_sums(own_hot, kernel)
    b2, b2_hot = unpack(b2_ref)
    kernel = kernel_tile(b2, y)
    for_2_out[...] = left_sums(y_hot, kernel)
    for_y_out[...] += right_sums(b2_hot, kernel)
    for_m2_out[...] = jnp.zeros_like(for_m2_out)

    @pl.when(even_ref[0] == 1)
    def _():
        bm2, bm2_hot = unpack(bm2_ref)
        kernel = kernel_tile(bm2, y)
        for_m2_out[...] = left_sums(y_hot, kernel)
        for_y_out[...] += right_sums(bm2_hot, kernel)


def late_body(
    even_ref, bm2_ref, b4_ref, y_top_ref, y_end_ref, for_y_in, for_m2_out, for_4_out, for_y_out
):
    b4, b4_hot = unpack(b4_ref)
    bm2, bm2_hot = unpack(bm2_ref)
    kernel = kernel_tile(bm2, b4)
    for_m2_out[...] = left_sums(b4_hot, kernel)
    for_4_out[...] = right_sums(bm2_hot, kernel)
    for_y_out[...] = for_y_in[...]

    @pl.when(even_ref[0] == 0)
    def _():
        y, y_hot = unpack(jnp.concatenate([y_top_ref[...], y_end_ref[...]], axis=0))
        kernel = kernel_tile(b4, y)
        for_4_out[...] += left_sums(y_hot, kernel)
        for_y_out[...] += right_sums(b4_hot, kernel)


def choose_body(even_ref, b2_ref, bm2_ref, top_out, end_out):
    cut = top_out.shape[0]

    @pl.when(even_ref[0] == 1)
    def _():
        top_out[...] = b2_ref[:cut, :]
        end_out[...] = b2_ref[cut:, :]

    @pl.when(even_ref[0] == 0)
    def _():
        top_out[...] = bm2_ref[:cut, :]
        end_out[...] = bm2_ref[cut:, :]


def call(body, shapes, *args, moved=1000):
    vmem = pl.BlockSpec(memory_space=pltpu.VMEM)
    smem = pl.BlockSpec(memory_space=pltpu.SMEM)
    return pl.pallas_call(
        body,
        out_shape=[pltpu.VMEM(shape, jnp.float32) for shape in shapes],
        in_specs=[smem if a.ndim == 1 else vmem for a in args],
        out_specs=[vmem] * len(shapes),
        compiler_params=pltpu.CompilerParams(vmem_limit_bytes=16 * 2**20),
        cost_estimate=pl.CostEstimate(flops=1000, bytes_accessed=moved, transcendentals=0),
    )(*(a if a.ndim == 1 else pltpu.with_memory_space_constraint(a, pltpu.VMEM) for a in args))


def on_device(embeddings, labels):
    rows, dim = embeddings.shape
    cut = TOP + rows // 2
    sums = (CLUSTERS, rows)
    even = (1 - lax.axis_index("blk") % 2).astype(jnp.int32)[None]
    own = pack(embeddings, labels)

    b2 = pull(own)
    bm2 = push(own)
    (own_0,) = call(self_body, [sums], own, moved=4 * own.size)
    b2, own_0 = lax.optimization_barrier((b2, own_0))
    own_2, for_2 = call(pair_body, [sums] * 2, own, b2, moved=8 * own.size)
    b2, own_2, for_2 = lax.optimization_barrier((b2, own_2, for_2))
    b4 = pull(b2)

    b2, bm2 = lax.optimization_barrier((b2, bm2))
    y_top, y_end = call(
        choose_body, [(cut, dim), (rows + TOP - cut, dim)], even, b2, bm2, moved=8 * own.size
    )
    y = swap(y_top), swap(y_end)
    for_m2, for_2_m2 = call(pair_body, [sums] * 2, bm2, b2, moved=8 * own.size)

    y, for_m2, for_2_m2 = lax.optimization_barrier((y, for_m2, for_2_m2))
    own_y, for_m2_y, for_2_y, for_y = call(
        visitor_body, [sums] * 4, even, own, bm2, b2, *y, moved=8 * own.size
    )
    back_m2 = give(for_y, 0)

    b4, own_y, for_m2_y, for_2_y, for_y = lax.optimization_barrier(
        (b4, own_y, for_m2_y, for_2_y, for_y)
    )
    for_m2_4, for_4, for_y = call(
        late_body, [sums] * 3, even, bm2, b4, *y, for_y, moved=16 * own.size
    )
    home_4 = push(for_4, chips=2)
    home_m2 = pull(for_m2 + for_m2_y + for_m2_4 + back_m2)
    back_2 = give(for_y, 1)
    home_2 = push(for_2 + for_2_m2 + for_2_y + back_2)
    own, home_m2, home_2 = lax.optimization_barrier(
        (own_0 + own_2 + own_y + home_4, home_m2, home_2)
    )
    return (own + home_m2 + home_2).T


def solution(mesh):
    placed = (P("blk", None), P("blk"))
    return jax.shard_map(
        on_device, mesh=mesh, in_specs=placed, out_specs=P("blk", None), check_vma=False
    )
```

```python
import jax
import jax.numpy as jnp
from jax import lax
from jax.experimental import pallas as pl
from jax.experimental.pallas import tpu as pltpu
from jax.sharding import PartitionSpec as P

CLUSTERS = 256
TOP = 8


def even_odd(n, even, odd):
    return [(i, (i + (even if i % 2 == 0 else odd)) % n) for i in range(n)]


def pull(value):
    n = lax.axis_size("blk")
    return lax.ppermute(value, "blk", even_odd(n, -2, 2))


def push(value):
    n = lax.axis_size("blk")
    return lax.ppermute(value, "blk", even_odd(n, 2, -2))


def swap(value):
    n = lax.axis_size("blk")
    return lax.ppermute(value, "blk", even_odd(n, 1, -1))


def give(value, core):
    n = lax.axis_size("blk")
    return lax.ppermute(value, "blk", [(i, i ^ 1) for i in range(core, n, 2)])


def one_hot(labels):
    cluster = lax.broadcasted_iota(jnp.int32, (CLUSTERS, labels.shape[1]), 0)
    return jnp.where(cluster == labels.astype(jnp.int32), 1.0, 0.0).astype(jnp.bfloat16)


def unpack(message):
    rows = message[TOP:, :]
    high = rows.astype(jnp.bfloat16)
    low = (rows - high.astype(jnp.float32)).astype(jnp.bfloat16)
    kept = high.astype(jnp.float32) + low.astype(jnp.float32)
    norms = jnp.sum(kept * kept, axis=1, keepdims=True)
    return (high, low, norms), one_hot(message[0:1, : rows.shape[0]])


def pack_body(embeddings_ref, labels_ref, message_ref, held, done):
    rows = embeddings_ref.shape[0]
    copy = pltpu.make_async_copy(embeddings_ref, message_ref.at[pl.ds(TOP, rows)], done.at[0])
    copy.start()
    labels = pltpu.make_async_copy(labels_ref, held, done.at[1])
    labels.start()
    message_ref[:TOP, :] = jnp.zeros((TOP, message_ref.shape[1]), jnp.float32)
    labels.wait()
    message_ref[0:1, :rows] = held[...].astype(jnp.float32)
    copy.wait()


def pack(embeddings, labels):
    rows, dim = embeddings.shape
    return pl.pallas_call(
        pack_body,
        out_shape=pltpu.VMEM((TOP + rows, dim), jnp.float32),
        in_specs=[pl.BlockSpec(memory_space=pltpu.HBM)] * 2,
        out_specs=pl.BlockSpec(memory_space=pltpu.VMEM),
        scratch_shapes=[pltpu.VMEM((1, rows), jnp.int32), pltpu.SemaphoreType.DMA((2,))],
        compiler_params=pltpu.CompilerParams(vmem_limit_bytes=16 * 2**20),
    )(
        pltpu.with_memory_space_constraint(embeddings, pltpu.HBM),
        pltpu.with_memory_space_constraint(labels[None, :], pltpu.HBM),
    )


def kernel_tile(left, right):
    high, low, left_norms = left
    left = jnp.concatenate([high, low], axis=1)
    high, low, right_norms = right
    right_norms = jnp.transpose(jnp.broadcast_to(right_norms, (high.shape[0], 128)))[0:1, :]
    inner = sum(
        lax.dot_general(
            left,
            jnp.concatenate(parts, axis=1),
            (((1,), (1,)), ((), ())),
            preferred_element_type=jnp.float32,
        )
        for parts in ((low, high), (high, low))
    )
    return jnp.exp(-(left_norms + right_norms - 2.0 * inner)).astype(jnp.bfloat16)


def left_sums(right_hot, kernel):
    return lax.dot_general(
        right_hot, kernel, (((1,), (1,)), ((), ())), preferred_element_type=jnp.float32
    )


def right_sums(left_hot, kernel):
    return jnp.dot(left_hot, kernel, preferred_element_type=jnp.float32)


def self_body(own_ref, own_out):
    own, own_hot = unpack(own_ref)
    own_out[...] = left_sums(own_hot, kernel_tile(own, own))


def pair_body(own_ref, bm2_ref, b2_ref, own_out, for_m2_out, for_2_out):
    b2, b2_hot = unpack(b2_ref)
    bm2, bm2_hot = unpack(bm2_ref)
    kernel = kernel_tile(bm2, b2)
    for_m2_out[...] = left_sums(b2_hot, kernel)
    for_2_out[...] = right_sums(bm2_hot, kernel)
    own, own_hot = unpack(own_ref)
    kernel = kernel_tile(own, b2)
    own_out[...] = left_sums(b2_hot, kernel)
    for_2_out[...] += right_sums(own_hot, kernel)


def visitor_body(
    even_ref, own_ref, bm2_ref, b2_ref, y_top_ref, y_end_ref,
    own_out, for_m2_out, for_2_out, for_y_out,
):
    y, y_hot = unpack(jnp.concatenate([y_top_ref[...], y_end_ref[...]], axis=0))
    own, own_hot = unpack(own_ref)
    kernel = kernel_tile(own, y)
    own_out[...] = left_sums(y_hot, kernel)
    for_y_out[...] = right_sums(own_hot, kernel)
    b2, b2_hot = unpack(b2_ref)
    kernel = kernel_tile(b2, y)
    for_2_out[...] = left_sums(y_hot, kernel)
    for_y_out[...] += right_sums(b2_hot, kernel)
    for_m2_out[...] = jnp.zeros_like(for_m2_out)

    @pl.when(even_ref[0] == 1)
    def _():
        bm2, bm2_hot = unpack(bm2_ref)
        kernel = kernel_tile(bm2, y)
        for_m2_out[...] = left_sums(y_hot, kernel)
        for_y_out[...] += right_sums(bm2_hot, kernel)


def late_body(
    even_ref, bm2_ref, b4_ref, y_top_ref, y_end_ref, for_y_in, for_m2_out, for_4_out, for_y_out
):
    b4, b4_hot = unpack(b4_ref)
    bm2, bm2_hot = unpack(bm2_ref)
    kernel = kernel_tile(bm2, b4)
    for_m2_out[...] = left_sums(b4_hot, kernel)
    for_4_out[...] = right_sums(bm2_hot, kernel)
    for_y_out[...] = for_y_in[...]

    @pl.when(even_ref[0] == 0)
    def _():
        y, y_hot = unpack(jnp.concatenate([y_top_ref[...], y_end_ref[...]], axis=0))
        kernel = kernel_tile(b4, y)
        for_4_out[...] += left_sums(y_hot, kernel)
        for_y_out[...] += right_sums(b4_hot, kernel)


def choose_body(even_ref, b2_ref, bm2_ref, top_out, end_out):
    cut = top_out.shape[0]

    @pl.when(even_ref[0] == 1)
    def _():
        top_out[...] = b2_ref[:cut, :]
        end_out[...] = b2_ref[cut:, :]

    @pl.when(even_ref[0] == 0)
    def _():
        top_out[...] = bm2_ref[:cut, :]
        end_out[...] = bm2_ref[cut:, :]


def call(body, shapes, *args, moved=1000):
    vmem = pl.BlockSpec(memory_space=pltpu.VMEM)
    smem = pl.BlockSpec(memory_space=pltpu.SMEM)
    return pl.pallas_call(
        body,
        out_shape=[pltpu.VMEM(shape, jnp.float32) for shape in shapes],
        in_specs=[smem if a.ndim == 1 else vmem for a in args],
        out_specs=[vmem] * len(shapes),
        compiler_params=pltpu.CompilerParams(vmem_limit_bytes=16 * 2**20),
        cost_estimate=pl.CostEstimate(flops=1000, bytes_accessed=moved, transcendentals=0),
    )(*(a if a.ndim == 1 else pltpu.with_memory_space_constraint(a, pltpu.VMEM) for a in args))


def on_device(embeddings, labels):
    rows, dim = embeddings.shape
    cut = TOP + rows // 2
    sums = (CLUSTERS, rows)
    even = (1 - lax.axis_index("blk") % 2).astype(jnp.int32)[None]
    own, even = lax.optimization_barrier((pack(embeddings, labels), even))

    b2 = pull(own)
    bm2 = push(own)
    (own_0,) = call(self_body, [sums], own, moved=4 * own.size)
    b2, own_0 = lax.optimization_barrier((b2, own_0))
    b4 = pull(b2)

    b2, bm2 = lax.optimization_barrier((b2, bm2))
    y_top, y_end = call(
        choose_body, [(cut, dim), (rows + TOP - cut, dim)], even, b2, bm2, moved=8 * own.size
    )
    y = swap(y_top), swap(y_end)
    own_2, for_m2, for_2 = call(pair_body, [sums] * 3, own, bm2, b2, moved=16 * own.size)

    y, own_2, for_m2, for_2 = lax.optimization_barrier((y, own_2, for_m2, for_2))
    own_y, for_m2_y, for_2_y, for_y = call(
        visitor_body, [sums] * 4, even, own, bm2, b2, *y, moved=8 * own.size
    )
    back_m2 = give(for_y, 0)

    b4, own_y, for_m2_y, for_2_y, for_y = lax.optimization_barrier(
        (b4, own_y, for_m2_y, for_2_y, for_y)
    )
    for_m2_4, for_4, for_y = call(
        late_body, [sums] * 3, even, bm2, b4, *y, for_y, moved=16 * own.size
    )
    back_4 = push(for_4)
    home_m2 = pull(for_m2 + for_m2_y + for_m2_4 + back_m2)
    back_2 = give(for_y, 1)
    back_4, back_2, for_2 = lax.optimization_barrier((back_4, back_2, for_2 + for_2_y))
    home_2 = push(for_2 + back_2 + back_4)
    return (own_0 + own_2 + own_y + home_m2 + home_2).T


def solution(mesh):
    placed = (P("blk", None), P("blk"))
    return jax.shard_map(
        on_device, mesh=mesh, in_specs=placed, out_specs=P("blk", None), check_vma=False
    )
```

```python
import jax
import jax.numpy as jnp
from jax import lax
from jax.experimental import pallas as pl
from jax.experimental.pallas import tpu as pltpu
from jax.sharding import PartitionSpec as P

CLUSTERS = 256
ROWS = 512
DIM = 768
SUMS = ((CLUSTERS, ROWS), jnp.float32)
SPLIT = ((ROWS, 2 * DIM), jnp.bfloat16), ((ROWS, 128), jnp.float32)
TOP = 8


def even_odd(n, even, odd):
    return [(i, (i + (even if i % 2 == 0 else odd)) % n) for i in range(n)]


def pull(value):
    n = lax.axis_size("blk")
    return lax.ppermute(value, "blk", even_odd(n, -2, 2))


def push(value):
    n = lax.axis_size("blk")
    return lax.ppermute(value, "blk", even_odd(n, 2, -2))


def swap(value):
    n = lax.axis_size("blk")
    return lax.ppermute(value, "blk", even_odd(n, 1, -1))


def give(value, core):
    n = lax.axis_size("blk")
    return lax.ppermute(value, "blk", [(i, i ^ 1) for i in range(core, n, 2)])


def one_hot(labels):
    cluster = lax.broadcasted_iota(jnp.int32, (CLUSTERS, labels.shape[1]), 0)
    return jnp.where(cluster == labels.astype(jnp.int32), 1.0, 0.0).astype(jnp.bfloat16)


def labels_of(message_ref):
    return one_hot(message_ref[0:1, :ROWS])


def split(message, parts_out, norms_out):
    rows = message[TOP:, :]
    dim = rows.shape[1]
    high = rows.astype(jnp.bfloat16)
    low = (rows - high.astype(jnp.float32)).astype(jnp.bfloat16)
    kept = high.astype(jnp.float32) + low.astype(jnp.float32)
    parts_out[:, :dim] = high
    parts_out[:, dim:] = low
    norms_out[...] = jnp.broadcast_to(jnp.sum(kept * kept, axis=1, keepdims=True), norms_out.shape)


def pack_body(embeddings_ref, labels_ref, message_ref, held, done):
    rows = embeddings_ref.shape[0]
    copy = pltpu.make_async_copy(embeddings_ref, message_ref.at[pl.ds(TOP, rows)], done.at[0])
    copy.start()
    labels = pltpu.make_async_copy(labels_ref, held, done.at[1])
    labels.start()
    message_ref[:TOP, :] = jnp.zeros((TOP, message_ref.shape[1]), jnp.float32)
    labels.wait()
    message_ref[0:1, :rows] = held[...].astype(jnp.float32)
    copy.wait()


def pack(embeddings, labels):
    rows, dim = embeddings.shape
    return pl.pallas_call(
        pack_body,
        out_shape=pltpu.VMEM((TOP + rows, dim), jnp.float32),
        in_specs=[pl.BlockSpec(memory_space=pltpu.HBM)] * 2,
        out_specs=pl.BlockSpec(memory_space=pltpu.VMEM),
        scratch_shapes=[pltpu.VMEM((1, rows), jnp.int32), pltpu.SemaphoreType.DMA((2,))],
        compiler_params=pltpu.CompilerParams(vmem_limit_bytes=16 * 2**20),
    )(
        pltpu.with_memory_space_constraint(embeddings, pltpu.HBM),
        pltpu.with_memory_space_constraint(labels[None, :], pltpu.HBM),
    )


def kernel_tile(left, left_norms, right, right_norms):
    dim = right.shape[1] // 2
    swapped = jnp.concatenate([right[:, dim:], right[:, :dim]], axis=1)
    inner = sum(
        lax.dot_general(
            left[...], parts, (((1,), (1,)), ((), ())), preferred_element_type=jnp.float32
        )
        for parts in (swapped, right[...])
    )
    right_norms = jnp.transpose(right_norms[...])[0:1, :]
    return jnp.exp(-(left_norms[:, 0:1] + right_norms - 2.0 * inner)).astype(jnp.bfloat16)


def left_sums(right_hot, kernel):
    return lax.dot_general(
        right_hot, kernel, (((1,), (1,)), ((), ())), preferred_element_type=jnp.float32
    )


def right_sums(left_hot, kernel):
    return jnp.dot(left_hot, kernel, preferred_element_type=jnp.float32)


def self_body(own_ref, own_out, parts, norms):
    split(own_ref, parts, norms)
    own_out[...] = left_sums(labels_of(own_ref), kernel_tile(parts, norms, parts, norms))


def pair_body(
    own_ref, own_parts, own_norms, bm2_ref, b2_ref,
    own_out, for_m2_out, for_2_out, bm2_parts, bm2_norms, b2_parts, b2_norms,
):
    split(b2_ref, b2_parts, b2_norms)
    split(bm2_ref, bm2_parts, bm2_norms)
    b2_hot = labels_of(b2_ref)
    kernel = kernel_tile(bm2_parts, bm2_norms, b2_parts, b2_norms)
    for_m2_out[...] = left_sums(b2_hot, kernel)
    for_2_out[...] = right_sums(labels_of(bm2_ref), kernel)
    kernel = kernel_tile(own_parts, own_norms, b2_parts, b2_norms)
    own_out[...] = left_sums(b2_hot, kernel)
    for_2_out[...] += right_sums(labels_of(own_ref), kernel)


def visitor_body(
    even_ref, own_ref, own_parts, own_norms, bm2_ref, bm2_parts, bm2_norms,
    b2_ref, b2_parts, b2_norms, y_top_ref, y_end_ref,
    own_out, for_m2_out, for_2_out, for_y_out, y_parts, y_norms,
):
    split(jnp.concatenate([y_top_ref[...], y_end_ref[...]], axis=0), y_parts, y_norms)
    y_hot = labels_of(y_top_ref)
    kernel = kernel_tile(own_parts, own_norms, y_parts, y_norms)
    own_out[...] = left_sums(y_hot, kernel)
    for_y_out[...] = right_sums(labels_of(own_ref), kernel)
    kernel = kernel_tile(b2_parts, b2_norms, y_parts, y_norms)
    for_2_out[...] = left_sums(y_hot, kernel)
    for_y_out[...] += right_sums(labels_of(b2_ref), kernel)
    for_m2_out[...] = jnp.zeros_like(for_m2_out)

    @pl.when(even_ref[0] == 1)
    def _():
        kernel = kernel_tile(bm2_parts, bm2_norms, y_parts, y_norms)
        for_m2_out[...] = left_sums(y_hot, kernel)
        for_y_out[...] += right_sums(labels_of(bm2_ref), kernel)


def late_body(
    even_ref, bm2_ref, bm2_parts, bm2_norms, b4_ref, y_top_ref, y_parts, y_norms, for_y_in,
    for_m2_out, for_4_out, for_y_out, b4_parts, b4_norms,
):
    split(b4_ref, b4_parts, b4_norms)
    b4_hot = labels_of(b4_ref)
    kernel = kernel_tile(bm2_parts, bm2_norms, b4_parts, b4_norms)
    for_m2_out[...] = left_sums(b4_hot, kernel)
    for_4_out[...] = right_sums(labels_of(bm2_ref), kernel)
    for_y_out[...] = for_y_in[...]

    @pl.when(even_ref[0] == 0)
    def _():
        kernel = kernel_tile(b4_parts, b4_norms, y_parts, y_norms)
        for_4_out[...] += left_sums(labels_of(y_top_ref), kernel)
        for_y_out[...] += right_sums(b4_hot, kernel)


def choose_body(even_ref, b2_ref, bm2_ref, top_out, end_out):
    cut = top_out.shape[0]

    @pl.when(even_ref[0] == 1)
    def _():
        top_out[...] = b2_ref[:cut, :]
        end_out[...] = b2_ref[cut:, :]

    @pl.when(even_ref[0] == 0)
    def _():
        top_out[...] = bm2_ref[:cut, :]
        end_out[...] = bm2_ref[cut:, :]


def call(body, outs, *args, scratch=(), moved=1000):
    vmem = pl.BlockSpec(memory_space=pltpu.VMEM)
    smem = pl.BlockSpec(memory_space=pltpu.SMEM)
    return pl.pallas_call(
        body,
        out_shape=[pltpu.VMEM(*out) for out in outs],
        in_specs=[smem if a.ndim == 1 else vmem for a in args],
        out_specs=[vmem] * len(outs),
        scratch_shapes=[pltpu.VMEM(*shape) for shape in scratch],
        compiler_params=pltpu.CompilerParams(vmem_limit_bytes=16 * 2**20),
        cost_estimate=pl.CostEstimate(flops=1000, bytes_accessed=moved, transcendentals=0),
    )(*(a if a.ndim == 1 else pltpu.with_memory_space_constraint(a, pltpu.VMEM) for a in args))


def on_device(embeddings, labels):
    cut = TOP + ROWS // 2
    even = (1 - lax.axis_index("blk") % 2).astype(jnp.int32)[None]
    own, even = lax.optimization_barrier((pack(embeddings, labels), even))

    b2 = pull(own)
    bm2 = push(own)
    own_0, *own_split = call(self_body, [SUMS, *SPLIT], own, moved=4 * own.size)
    b2, own_0 = lax.optimization_barrier((b2, own_0))
    b4 = pull(b2)

    b2, bm2 = lax.optimization_barrier((b2, bm2))
    pieces = [((rows, DIM), jnp.float32) for rows in (cut, TOP + ROWS - cut)]
    y_top, y_end = call(choose_body, pieces, even, b2, bm2, moved=8 * own.size)
    y = swap(y_top), swap(y_end)
    own_2, for_m2, for_2, *splits = call(
        pair_body, [SUMS] * 3 + [*SPLIT] * 2, own, *own_split, bm2, b2, moved=16 * own.size
    )
    bm2_split, b2_split = splits[:2], splits[2:]

    y, own_2, for_m2, for_2 = lax.optimization_barrier((y, own_2, for_m2, for_2))
    own_y, for_m2_y, for_2_y, for_y, *y_split = call(
        visitor_body, [SUMS] * 4 + [*SPLIT],
        even, own, *own_split, bm2, *bm2_split, b2, *b2_split, *y, moved=8 * own.size,
    )
    back_m2 = give(for_y, 0)

    b4, own_y, for_m2_y, for_2_y, for_y = lax.optimization_barrier(
        (b4, own_y, for_m2_y, for_2_y, for_y)
    )
    for_m2_4, for_4, for_y = call(
        late_body, [SUMS] * 3, even, bm2, *bm2_split, b4, y[0], *y_split, for_y,
        scratch=SPLIT, moved=16 * own.size,
    )
    back_4 = push(for_4)
    home_m2 = pull(for_m2 + for_m2_y + for_m2_4 + back_m2)
    back_2 = give(for_y, 1)
    back_4, back_2, for_2 = lax.optimization_barrier((back_4, back_2, for_2 + for_2_y))
    home_2 = push(for_2 + back_2 + back_4)
    return (own_0 + own_2 + own_y + home_m2 + home_2).T


def solution(mesh):
    placed = (P("blk", None), P("blk"))
    return jax.shard_map(
        on_device, mesh=mesh, in_specs=placed, out_specs=P("blk", None), check_vma=False
    )
```

```python
import jax
import jax.numpy as jnp
from jax import lax
from jax.experimental import pallas as pl
from jax.experimental.pallas import tpu as pltpu
from jax.sharding import PartitionSpec as P

CLUSTERS = 256
ROWS = 512
DIM = 768
TOP = 8
SUMS = ((CLUSTERS, ROWS), jnp.float32)
SPLIT = ((ROWS, 2 * DIM), jnp.bfloat16), ((ROWS, 128), jnp.float32)
PIECES = ((TOP + ROWS // 2, DIM), jnp.float32), ((ROWS // 2, DIM), jnp.float32)


def even_odd(n, even, odd):
    return [(i, (i + (even if i % 2 == 0 else odd)) % n) for i in range(n)]


def pull(value):
    n = lax.axis_size("blk")
    return lax.ppermute(value, "blk", even_odd(n, -2, 2))


def push(value):
    n = lax.axis_size("blk")
    return lax.ppermute(value, "blk", even_odd(n, 2, -2))


def swap(value):
    n = lax.axis_size("blk")
    return lax.ppermute(value, "blk", even_odd(n, 1, -1))


def give(value, core):
    n = lax.axis_size("blk")
    return lax.ppermute(value, "blk", [(i, i ^ 1) for i in range(core, n, 2)])


def one_hot(labels):
    cluster = lax.broadcasted_iota(jnp.int32, (CLUSTERS, labels.shape[1]), 0)
    return jnp.where(cluster == labels.astype(jnp.int32), 1.0, 0.0).astype(jnp.bfloat16)


def labels_of(message_ref):
    return one_hot(message_ref[0:1, :ROWS])


def split(message, parts_out, norms_out):
    rows = message[TOP:, :]
    dim = rows.shape[1]
    high = rows.astype(jnp.bfloat16)
    low = (rows - high.astype(jnp.float32)).astype(jnp.bfloat16)
    kept = high.astype(jnp.float32) + low.astype(jnp.float32)
    parts_out[:, :dim] = high
    parts_out[:, dim:] = low
    norms_out[...] = jnp.broadcast_to(jnp.sum(kept * kept, axis=1, keepdims=True), norms_out.shape)


def pack_body(embeddings_ref, labels_ref, message_ref, top_ref, end_ref, held, done):
    rows = top_ref.shape[0] - TOP
    whole = pltpu.make_async_copy(
        embeddings_ref, message_ref.at[pl.ds(TOP, ROWS)], done.at[0]
    )
    first = pltpu.make_async_copy(
        embeddings_ref.at[pl.ds(0, rows)], top_ref.at[pl.ds(TOP, rows)], done.at[1]
    )
    second = pltpu.make_async_copy(
        embeddings_ref.at[pl.ds(rows, ROWS - rows)], end_ref, done.at[2]
    )
    labels = pltpu.make_async_copy(labels_ref, held, done.at[3])
    labels.start()
    whole.start()
    first.start()
    second.start()
    top = jnp.zeros((TOP, DIM), jnp.float32)
    message_ref[:TOP, :] = top
    top_ref[:TOP, :] = top
    labels.wait()
    row = held[...].astype(jnp.float32)
    message_ref[0:1, :ROWS] = row
    top_ref[0:1, :ROWS] = row
    whole.wait()
    first.wait()
    second.wait()


def pack(embeddings, labels):
    shapes = ((TOP + ROWS, DIM), jnp.float32), *PIECES
    return pl.pallas_call(
        pack_body,
        out_shape=[pltpu.VMEM(*shape) for shape in shapes],
        in_specs=[pl.BlockSpec(memory_space=pltpu.HBM)] * 2,
        out_specs=[pl.BlockSpec(memory_space=pltpu.VMEM)] * 3,
        scratch_shapes=[pltpu.VMEM((1, ROWS), jnp.int32), pltpu.SemaphoreType.DMA((4,))],
        compiler_params=pltpu.CompilerParams(vmem_limit_bytes=16 * 2**20),
    )(
        pltpu.with_memory_space_constraint(embeddings, pltpu.HBM),
        pltpu.with_memory_space_constraint(labels[None, :], pltpu.HBM),
    )


def kernel_tile(left, left_norms, right, right_norms):
    dim = right.shape[1] // 2
    swapped = jnp.concatenate([right[:, dim:], right[:, :dim]], axis=1)
    inner = sum(
        lax.dot_general(
            left[...], parts, (((1,), (1,)), ((), ())), preferred_element_type=jnp.float32
        )
        for parts in (swapped, right[...])
    )
    right_norms = jnp.transpose(right_norms[...])[0:1, :]
    return jnp.exp(-(left_norms[:, 0:1] + right_norms - 2.0 * inner)).astype(jnp.bfloat16)


def left_sums(right_hot, kernel):
    return lax.dot_general(
        right_hot, kernel, (((1,), (1,)), ((), ())), preferred_element_type=jnp.float32
    )


def right_sums(left_hot, kernel):
    return jnp.dot(left_hot, kernel, preferred_element_type=jnp.float32)


def split_pieces(top_ref, end_ref, parts, norms):
    split(jnp.concatenate([top_ref[...], end_ref[...]], axis=0), parts, norms)


def self_body(own_ref, own_out, parts, norms):
    split(own_ref, parts, norms)
    own_out[...] = left_sums(labels_of(own_ref), kernel_tile(parts, norms, parts, norms))


def chip_body(
    even_ref, own_ref, own_parts, own_norms, top_ref, end_ref, own_in,
    own_out, for_1_out, parts, norms,
):
    own_out[...] = own_in[...]

    @pl.when(even_ref[0] == 1)
    def _():
        split_pieces(top_ref, end_ref, parts, norms)
        kernel = kernel_tile(own_parts, own_norms, parts, norms)
        own_out[...] += left_sums(labels_of(top_ref), kernel)
        for_1_out[...] = right_sums(labels_of(own_ref), kernel)

    @pl.when(even_ref[0] == 0)
    def _():
        for_1_out[...] = jnp.zeros_like(for_1_out)


def pair_body(
    own_ref, own_parts, own_norms, bm2_ref, b2_ref,
    own_out, for_m2_out, for_2_out, bm2_parts, bm2_norms, b2_parts, b2_norms,
):
    split(b2_ref, b2_parts, b2_norms)
    split(bm2_ref, bm2_parts, bm2_norms)
    b2_hot = labels_of(b2_ref)
    kernel = kernel_tile(bm2_parts, bm2_norms, b2_parts, b2_norms)
    for_m2_out[...] = left_sums(b2_hot, kernel)
    for_2_out[...] = right_sums(labels_of(bm2_ref), kernel)
    kernel = kernel_tile(own_parts, own_norms, b2_parts, b2_norms)
    own_out[...] = left_sums(b2_hot, kernel)
    for_2_out[...] += right_sums(labels_of(own_ref), kernel)


def visitor_body(
    even_ref, own_ref, own_parts, own_norms, bm2_ref, bm2_parts, bm2_norms,
    b2_ref, b2_parts, b2_norms, y_top_ref, y_end_ref,
    own_out, for_m2_out, for_2_out, for_y_out, y_parts, y_norms,
):
    split_pieces(y_top_ref, y_end_ref, y_parts, y_norms)
    y_hot = labels_of(y_top_ref)
    kernel = kernel_tile(own_parts, own_norms, y_parts, y_norms)
    own_out[...] = left_sums(y_hot, kernel)
    for_y_out[...] = right_sums(labels_of(own_ref), kernel)

    @pl.when(even_ref[0] == 1)
    def _():
        kernel = kernel_tile(bm2_parts, bm2_norms, y_parts, y_norms)
        for_m2_out[...] = left_sums(y_hot, kernel)
        for_2_out[...] = jnp.zeros_like(for_2_out)
        for_y_out[...] += right_sums(labels_of(bm2_ref), kernel)

    @pl.when(even_ref[0] == 0)
    def _():
        kernel = kernel_tile(b2_parts, b2_norms, y_parts, y_norms)
        for_2_out[...] = left_sums(y_hot, kernel)
        for_m2_out[...] = jnp.zeros_like(for_m2_out)
        for_y_out[...] += right_sums(labels_of(b2_ref), kernel)


def late_body(
    even_ref, bm2_ref, bm2_parts, bm2_norms, b4_ref, y_top_ref, y_parts, y_norms, for_y_in,
    for_m2_out, for_4_out, for_y_out, b4_parts, b4_norms,
):
    split(b4_ref, b4_parts, b4_norms)
    b4_hot = labels_of(b4_ref)
    kernel = kernel_tile(bm2_parts, bm2_norms, b4_parts, b4_norms)
    for_m2_out[...] = left_sums(b4_hot, kernel)
    for_4_out[...] = right_sums(labels_of(bm2_ref), kernel)
    for_y_out[...] = for_y_in[...]

    @pl.when(even_ref[0] == 0)
    def _():
        kernel = kernel_tile(b4_parts, b4_norms, y_parts, y_norms)
        for_4_out[...] += left_sums(labels_of(y_top_ref), kernel)
        for_y_out[...] += right_sums(b4_hot, kernel)


def choose_body(even_ref, b2_ref, bm2_ref, top_out, end_out):
    cut = top_out.shape[0]

    @pl.when(even_ref[0] == 1)
    def _():
        top_out[...] = b2_ref[:cut, :]
        end_out[...] = b2_ref[cut:, :]

    @pl.when(even_ref[0] == 0)
    def _():
        top_out[...] = bm2_ref[:cut, :]
        end_out[...] = bm2_ref[cut:, :]


def call(body, outs, *args, scratch=(), moved=1000):
    vmem = pl.BlockSpec(memory_space=pltpu.VMEM)
    smem = pl.BlockSpec(memory_space=pltpu.SMEM)
    return pl.pallas_call(
        body,
        out_shape=[pltpu.VMEM(*out) for out in outs],
        in_specs=[smem if a.ndim == 1 else vmem for a in args],
        out_specs=[vmem] * len(outs),
        scratch_shapes=[pltpu.VMEM(*shape) for shape in scratch],
        compiler_params=pltpu.CompilerParams(vmem_limit_bytes=16 * 2**20),
        cost_estimate=pl.CostEstimate(flops=1000, bytes_accessed=moved, transcendentals=0),
    )(*(a if a.ndim == 1 else pltpu.with_memory_space_constraint(a, pltpu.VMEM) for a in args))


def on_device(embeddings, labels):
    even = (1 - lax.axis_index("blk") % 2).astype(jnp.int32)[None]
    (own, *own_pieces), even = lax.optimization_barrier((pack(embeddings, labels), even))

    b2 = pull(own)
    own_0, *own_split = call(self_body, [SUMS, *SPLIT], own, moved=4 * own.size)
    later_own, own_0 = lax.optimization_barrier((own, own_0))
    bm2 = push(later_own)
    sibling = [give(piece, 1) for piece in own_pieces]
    own_0, for_1 = call(
        chip_body, [SUMS] * 2, even, own, *own_split, *sibling, own_0,
        scratch=SPLIT, moved=8 * own.size,
    )
    back_1 = give(for_1, 0)
    b2, own_0, back_1 = lax.optimization_barrier((b2, own_0, back_1))
    b4 = pull(b2)

    b2, bm2 = lax.optimization_barrier((b2, bm2))
    y_top, y_end = call(choose_body, PIECES, even, b2, bm2, moved=8 * own.size)
    y = swap(y_top), swap(y_end)
    own_2, for_m2, for_2, *splits = call(
        pair_body, [SUMS] * 3 + [*SPLIT] * 2, own, *own_split, bm2, b2, moved=16 * own.size
    )
    bm2_split, b2_split = splits[:2], splits[2:]

    y, own_2, for_m2, for_2 = lax.optimization_barrier((y, own_2, for_m2, for_2))
    own_y, for_m2_y, for_2_y, for_y, *y_split = call(
        visitor_body, [SUMS] * 4 + [*SPLIT],
        even, own, *own_split, bm2, *bm2_split, b2, *b2_split, *y, moved=8 * own.size,
    )
    back_m2 = give(for_y, 0)

    b4, own_y, for_m2_y, for_2_y, for_y = lax.optimization_barrier(
        (b4, own_y, for_m2_y, for_2_y, for_y)
    )
    for_m2_4, for_4, for_y = call(
        late_body, [SUMS] * 3, even, bm2, *bm2_split, b4, y[0], *y_split, for_y,
        scratch=SPLIT, moved=16 * own.size,
    )
    back_4 = push(for_4)
    back_2 = give(for_y, 1)
    for_m2 = for_m2 + for_m2_y + for_m2_4 + back_m2
    back_4, back_2, for_2, for_m2 = lax.optimization_barrier(
        (back_4, back_2, for_2 + for_2_y, for_m2)
    )
    home_2 = push(for_2 + back_2 + back_4)
    home_m2 = pull(for_m2)
    return (own_0 + back_1 + own_2 + own_y + home_m2 + home_2).T


def solution(mesh):
    placed = (P("blk", None), P("blk"))
    return jax.shard_map(
        on_device, mesh=mesh, in_specs=placed, out_specs=P("blk", None), check_vma=False
    )
```

```python
import jax
import jax.numpy as jnp
from jax import lax
from jax.experimental import pallas as pl
from jax.experimental.pallas import tpu as pltpu
from jax.sharding import PartitionSpec as P

CLUSTERS = 256
ROWS = 512
DIM = 768
TOP = 8
SUMS = ((CLUSTERS, ROWS), jnp.float32)
SPLIT = ((ROWS, 2 * DIM), jnp.bfloat16), ((ROWS, 128), jnp.float32)
PIECES = ((TOP + ROWS // 2, DIM), jnp.float32), ((ROWS // 2, DIM), jnp.float32)


def even_odd(n, even, odd):
    return [(i, (i + (even if i % 2 == 0 else odd)) % n) for i in range(n)]


def pull(value):
    n = lax.axis_size("blk")
    return lax.ppermute(value, "blk", even_odd(n, -2, 2))


def push(value):
    n = lax.axis_size("blk")
    return lax.ppermute(value, "blk", even_odd(n, 2, -2))


def swap(value):
    n = lax.axis_size("blk")
    return lax.ppermute(value, "blk", even_odd(n, 1, -1))


def give(value, core):
    n = lax.axis_size("blk")
    return lax.ppermute(value, "blk", [(i, i ^ 1) for i in range(core, n, 2)])


def one_hot(labels):
    cluster = lax.broadcasted_iota(jnp.int32, (CLUSTERS, labels.shape[1]), 0)
    return jnp.where(cluster == labels.astype(jnp.int32), 1.0, 0.0).astype(jnp.bfloat16)


def labels_of(message_ref):
    return one_hot(message_ref[0:1, :ROWS])


def split(message, parts_out, norms_out):
    rows = message[TOP:, :]
    dim = rows.shape[1]
    high = rows.astype(jnp.bfloat16)
    low = (rows - high.astype(jnp.float32)).astype(jnp.bfloat16)
    kept = high.astype(jnp.float32) + low.astype(jnp.float32)
    parts_out[:, :dim] = high
    parts_out[:, dim:] = low
    norms_out[...] = jnp.broadcast_to(jnp.sum(kept * kept, axis=1, keepdims=True), norms_out.shape)


def pack_body(embeddings_ref, labels_ref, message_ref, top_ref, end_ref, held, done):
    rows = top_ref.shape[0] - TOP
    whole = pltpu.make_async_copy(
        embeddings_ref, message_ref.at[pl.ds(TOP, ROWS)], done.at[0]
    )
    first = pltpu.make_async_copy(
        embeddings_ref.at[pl.ds(0, rows)], top_ref.at[pl.ds(TOP, rows)], done.at[1]
    )
    second = pltpu.make_async_copy(
        embeddings_ref.at[pl.ds(rows, ROWS - rows)], end_ref, done.at[2]
    )
    labels = pltpu.make_async_copy(labels_ref, held, done.at[3])
    labels.start()
    whole.start()
    first.start()
    second.start()
    top = jnp.zeros((TOP, DIM), jnp.float32)
    message_ref[:TOP, :] = top
    top_ref[:TOP, :] = top
    labels.wait()
    row = held[...].astype(jnp.float32)
    message_ref[0:1, :ROWS] = row
    top_ref[0:1, :ROWS] = row
    whole.wait()
    first.wait()
    second.wait()


def pack(embeddings, labels):
    shapes = ((TOP + ROWS, DIM), jnp.float32), *PIECES
    return pl.pallas_call(
        pack_body,
        out_shape=[pltpu.VMEM(*shape) for shape in shapes],
        in_specs=[pl.BlockSpec(memory_space=pltpu.HBM)] * 2,
        out_specs=[pl.BlockSpec(memory_space=pltpu.VMEM)] * 3,
        scratch_shapes=[pltpu.VMEM((1, ROWS), jnp.int32), pltpu.SemaphoreType.DMA((4,))],
        compiler_params=pltpu.CompilerParams(vmem_limit_bytes=16 * 2**20),
    )(
        pltpu.with_memory_space_constraint(embeddings, pltpu.HBM),
        pltpu.with_memory_space_constraint(labels[None, :], pltpu.HBM),
    )


def kernel_tile(left, left_norms, right, right_norms):
    dim = right.shape[1] // 2
    swapped = jnp.concatenate([right[:, dim:], right[:, :dim]], axis=1)
    inner = sum(
        lax.dot_general(
            left[...], parts, (((1,), (1,)), ((), ())), preferred_element_type=jnp.float32
        )
        for parts in (swapped, right[...])
    )
    right_norms = jnp.transpose(right_norms[...])[0:1, :]
    return jnp.exp(-(left_norms[:, 0:1] + right_norms - 2.0 * inner)).astype(jnp.bfloat16)


def left_sums(right_hot, kernel):
    return lax.dot_general(
        right_hot, kernel, (((1,), (1,)), ((), ())), preferred_element_type=jnp.float32
    )


def right_sums(left_hot, kernel):
    return jnp.dot(left_hot, kernel, preferred_element_type=jnp.float32)


def split_pieces(top_ref, end_ref, parts, norms):
    split(jnp.concatenate([top_ref[...], end_ref[...]], axis=0), parts, norms)


def self_body(own_ref, own_out, parts, norms):
    split(own_ref, parts, norms)
    own_out[...] = left_sums(labels_of(own_ref), kernel_tile(parts, norms, parts, norms))


def chip_body(
    even_ref, own_ref, own_parts, own_norms, top_ref, end_ref, own_in,
    own_out, for_1_out, parts, norms,
):
    own_out[...] = own_in[...]

    @pl.when(even_ref[0] == 1)
    def _():
        split_pieces(top_ref, end_ref, parts, norms)
        kernel = kernel_tile(own_parts, own_norms, parts, norms)
        own_out[...] += left_sums(labels_of(top_ref), kernel)
        for_1_out[...] = right_sums(labels_of(own_ref), kernel)

    @pl.when(even_ref[0] == 0)
    def _():
        for_1_out[...] = jnp.zeros_like(for_1_out)


def near_body(own_ref, own_parts, own_norms, b2_ref, own_out, for_2_out, b2_parts, b2_norms):
    split(b2_ref, b2_parts, b2_norms)
    kernel = kernel_tile(own_parts, own_norms, b2_parts, b2_norms)
    own_out[...] = left_sums(labels_of(b2_ref), kernel)
    for_2_out[...] = right_sums(labels_of(own_ref), kernel)


def across_body(
    bm2_ref, b2_ref, b2_parts, b2_norms, for_2_in, for_m2_out, for_2_out, bm2_parts, bm2_norms
):
    split(bm2_ref, bm2_parts, bm2_norms)
    kernel = kernel_tile(bm2_parts, bm2_norms, b2_parts, b2_norms)
    for_m2_out[...] = left_sums(labels_of(b2_ref), kernel)
    for_2_out[...] = for_2_in[...] + right_sums(labels_of(bm2_ref), kernel)


def visitor_body(
    even_ref, own_ref, own_parts, own_norms, bm2_ref, bm2_parts, bm2_norms,
    b2_ref, b2_parts, b2_norms, y_top_ref, y_end_ref,
    own_out, for_m2_out, for_2_out, for_y_out, y_parts, y_norms,
):
    split_pieces(y_top_ref, y_end_ref, y_parts, y_norms)
    y_hot = labels_of(y_top_ref)
    kernel = kernel_tile(own_parts, own_norms, y_parts, y_norms)
    own_out[...] = left_sums(y_hot, kernel)
    for_y_out[...] = right_sums(labels_of(own_ref), kernel)

    @pl.when(even_ref[0] == 1)
    def _():
        kernel = kernel_tile(bm2_parts, bm2_norms, y_parts, y_norms)
        for_m2_out[...] = left_sums(y_hot, kernel)
        for_2_out[...] = jnp.zeros_like(for_2_out)
        for_y_out[...] += right_sums(labels_of(bm2_ref), kernel)

    @pl.when(even_ref[0] == 0)
    def _():
        kernel = kernel_tile(b2_parts, b2_norms, y_parts, y_norms)
        for_2_out[...] = left_sums(y_hot, kernel)
        for_m2_out[...] = jnp.zeros_like(for_m2_out)
        for_y_out[...] += right_sums(labels_of(b2_ref), kernel)


def late_body(
    even_ref, bm2_ref, bm2_parts, bm2_norms, b4_ref, y_top_ref, y_parts, y_norms, for_y_in,
    for_m2_out, for_4_out, for_y_out, b4_parts, b4_norms,
):
    split(b4_ref, b4_parts, b4_norms)
    b4_hot = labels_of(b4_ref)
    kernel = kernel_tile(bm2_parts, bm2_norms, b4_parts, b4_norms)
    for_m2_out[...] = left_sums(b4_hot, kernel)
    for_4_out[...] = right_sums(labels_of(bm2_ref), kernel)
    for_y_out[...] = for_y_in[...]

    @pl.when(even_ref[0] == 0)
    def _():
        kernel = kernel_tile(b4_parts, b4_norms, y_parts, y_norms)
        for_4_out[...] += left_sums(labels_of(y_top_ref), kernel)
        for_y_out[...] += right_sums(b4_hot, kernel)


def choose_body(even_ref, b2_ref, bm2_ref, top_out, end_out):
    cut = top_out.shape[0]

    @pl.when(even_ref[0] == 1)
    def _():
        top_out[...] = b2_ref[:cut, :]
        end_out[...] = b2_ref[cut:, :]

    @pl.when(even_ref[0] == 0)
    def _():
        top_out[...] = bm2_ref[:cut, :]
        end_out[...] = bm2_ref[cut:, :]


def call(body, outs, *args, scratch=(), moved=1000):
    vmem = pl.BlockSpec(memory_space=pltpu.VMEM)
    smem = pl.BlockSpec(memory_space=pltpu.SMEM)
    return pl.pallas_call(
        body,
        out_shape=[pltpu.VMEM(*out) for out in outs],
        in_specs=[smem if a.ndim == 1 else vmem for a in args],
        out_specs=[vmem] * len(outs),
        scratch_shapes=[pltpu.VMEM(*shape) for shape in scratch],
        compiler_params=pltpu.CompilerParams(vmem_limit_bytes=16 * 2**20),
        cost_estimate=pl.CostEstimate(flops=1000, bytes_accessed=moved, transcendentals=0),
    )(*(a if a.ndim == 1 else pltpu.with_memory_space_constraint(a, pltpu.VMEM) for a in args))


def on_device(embeddings, labels):
    even = (1 - lax.axis_index("blk") % 2).astype(jnp.int32)[None]
    (own, *own_pieces), even = lax.optimization_barrier((pack(embeddings, labels), even))

    b2 = pull(own)
    own_0, *own_split = call(self_body, [SUMS, *SPLIT], own, moved=4 * own.size)
    later_own, own_0 = lax.optimization_barrier((own, own_0))
    bm2 = push(later_own)
    sibling = [give(piece, 1) for piece in own_pieces]
    own_0, for_1 = call(
        chip_body, [SUMS] * 2, even, own, *own_split, *sibling, own_0,
        scratch=SPLIT, moved=8 * own.size,
    )
    back_1 = give(for_1, 0)
    b2, own_0, back_1 = lax.optimization_barrier((b2, own_0, back_1))
    b4 = pull(b2)

    own_2, for_2, *b2_split = call(
        near_body, [SUMS] * 2 + [*SPLIT], own, *own_split, b2, moved=8 * own.size
    )
    b2, bm2, for_2 = lax.optimization_barrier((b2, bm2, for_2))
    y_top, y_end = call(choose_body, PIECES, even, b2, bm2, moved=8 * own.size)
    y = swap(y_top), swap(y_end)
    for_m2, for_2, *bm2_split = call(
        across_body, [SUMS] * 2 + [*SPLIT], bm2, b2, *b2_split, for_2, moved=8 * own.size
    )

    y, own_2, for_m2, for_2 = lax.optimization_barrier((y, own_2, for_m2, for_2))
    own_y, for_m2_y, for_2_y, for_y, *y_split = call(
        visitor_body, [SUMS] * 4 + [*SPLIT],
        even, own, *own_split, bm2, *bm2_split, b2, *b2_split, *y, moved=8 * own.size,
    )
    back_m2 = give(for_y, 0)

    b4, own_y, for_m2_y, for_2_y, for_y = lax.optimization_barrier(
        (b4, own_y, for_m2_y, for_2_y, for_y)
    )
    for_m2_4, for_4, for_y = call(
        late_body, [SUMS] * 3, even, bm2, *bm2_split, b4, y[0], *y_split, for_y,
        scratch=SPLIT, moved=16 * own.size,
    )
    back_4 = push(for_4)
    home_m2 = pull(for_m2 + for_m2_y + for_m2_4 + back_m2)
    back_2 = give(for_y, 1)
    back_4, back_2, for_2 = lax.optimization_barrier((back_4, back_2, for_2 + for_2_y))
    home_2 = push(for_2 + back_2 + back_4)
    return (own_0 + back_1 + own_2 + own_y + home_m2 + home_2).T


def solution(mesh):
    placed = (P("blk", None), P("blk"))
    return jax.shard_map(
        on_device, mesh=mesh, in_specs=placed, out_specs=P("blk", None), check_vma=False
    )
```

```python
import jax
import jax.numpy as jnp
from jax import lax
from jax.experimental import pallas as pl
from jax.experimental.pallas import tpu as pltpu
from jax.sharding import PartitionSpec as P

CLUSTERS = 256
ROWS = 512
DIM = 768
TOP = 8
SUMS = ((CLUSTERS, ROWS), jnp.float32)
SPLIT = ((ROWS, 2 * DIM), jnp.bfloat16), ((ROWS, 128), jnp.float32)
PIECES = ((TOP + ROWS // 2, DIM), jnp.float32), ((ROWS // 2, DIM), jnp.float32)


def even_odd(n, even, odd):
    return [(i, (i + (even if i % 2 == 0 else odd)) % n) for i in range(n)]


def pull(value):
    n = lax.axis_size("blk")
    return lax.ppermute(value, "blk", even_odd(n, -2, 2))


def push(value):
    n = lax.axis_size("blk")
    return lax.ppermute(value, "blk", even_odd(n, 2, -2))


def swap(value):
    n = lax.axis_size("blk")
    return lax.ppermute(value, "blk", even_odd(n, 1, -1))


def give(value, core):
    n = lax.axis_size("blk")
    return lax.ppermute(value, "blk", [(i, i ^ 1) for i in range(core, n, 2)])


def one_hot(labels):
    cluster = lax.broadcasted_iota(jnp.int32, (CLUSTERS, labels.shape[1]), 0)
    return jnp.where(cluster == labels.astype(jnp.int32), 1.0, 0.0).astype(jnp.bfloat16)


def labels_of(message_ref):
    return one_hot(message_ref[0:1, :ROWS])


def split(message, parts_out, norms_out):
    rows = message[TOP:, :]
    dim = rows.shape[1]
    high = rows.astype(jnp.bfloat16)
    low = (rows - high.astype(jnp.float32)).astype(jnp.bfloat16)
    kept = high.astype(jnp.float32) + low.astype(jnp.float32)
    parts_out[:, :dim] = high
    parts_out[:, dim:] = low
    norms_out[...] = jnp.broadcast_to(jnp.sum(kept * kept, axis=1, keepdims=True), norms_out.shape)


def pack_body(embeddings_ref, labels_ref, message_ref, held, done):
    rows = embeddings_ref.shape[0]
    copy = pltpu.make_async_copy(embeddings_ref, message_ref.at[pl.ds(TOP, rows)], done.at[0])
    copy.start()
    labels = pltpu.make_async_copy(labels_ref, held, done.at[1])
    labels.start()
    message_ref[:TOP, :] = jnp.zeros((TOP, message_ref.shape[1]), jnp.float32)
    labels.wait()
    message_ref[0:1, :rows] = held[...].astype(jnp.float32)
    copy.wait()


def pack(embeddings, labels):
    rows, dim = embeddings.shape
    return pl.pallas_call(
        pack_body,
        out_shape=pltpu.VMEM((TOP + rows, dim), jnp.float32),
        in_specs=[pl.BlockSpec(memory_space=pltpu.HBM)] * 2,
        out_specs=pl.BlockSpec(memory_space=pltpu.VMEM),
        scratch_shapes=[pltpu.VMEM((1, rows), jnp.int32), pltpu.SemaphoreType.DMA((2,))],
        compiler_params=pltpu.CompilerParams(vmem_limit_bytes=16 * 2**20),
    )(
        pltpu.with_memory_space_constraint(embeddings, pltpu.HBM),
        pltpu.with_memory_space_constraint(labels[None, :], pltpu.HBM),
    )


def kernel_tile(left, left_norms, right, right_norms):
    dim = right.shape[1] // 2
    swapped = jnp.concatenate([right[:, dim:], right[:, :dim]], axis=1)
    inner = sum(
        lax.dot_general(
            left[...], parts, (((1,), (1,)), ((), ())), preferred_element_type=jnp.float32
        )
        for parts in (swapped, right[...])
    )
    right_norms = jnp.transpose(right_norms[...])[0:1, :]
    return jnp.exp(-(left_norms[:, 0:1] + right_norms - 2.0 * inner)).astype(jnp.bfloat16)


def left_sums(right_hot, kernel):
    return lax.dot_general(
        right_hot, kernel, (((1,), (1,)), ((), ())), preferred_element_type=jnp.float32
    )


def right_sums(left_hot, kernel):
    return jnp.dot(left_hot, kernel, preferred_element_type=jnp.float32)


def split_pieces(top_ref, end_ref, parts, norms):
    split(jnp.concatenate([top_ref[...], end_ref[...]], axis=0), parts, norms)


def self_body(own_ref, own_out, parts, norms, top_out, end_out):
    cut = top_out.shape[0]
    top_out[...] = own_ref[:cut, :]
    end_out[...] = own_ref[cut:, :]
    split(own_ref, parts, norms)
    own_out[...] = left_sums(labels_of(own_ref), kernel_tile(parts, norms, parts, norms))


def final_body(*refs):
    *parts, out = refs
    total = parts[0][...]
    for part in parts[1:]:
        total += part[...]
    out[...] = total.T


def chip_body(
    even_ref, own_ref, own_parts, own_norms, top_ref, end_ref, own_in,
    own_out, for_1_out, parts, norms,
):
    own_out[...] = own_in[...]

    @pl.when(even_ref[0] == 1)
    def _():
        split_pieces(top_ref, end_ref, parts, norms)
        kernel = kernel_tile(own_parts, own_norms, parts, norms)
        own_out[...] += left_sums(labels_of(top_ref), kernel)
        for_1_out[...] = right_sums(labels_of(own_ref), kernel)

    @pl.when(even_ref[0] == 0)
    def _():
        for_1_out[...] = jnp.zeros_like(for_1_out)


def near_body(own_ref, own_parts, own_norms, b2_ref, own_out, for_2_out, b2_parts, b2_norms):
    split(b2_ref, b2_parts, b2_norms)
    kernel = kernel_tile(own_parts, own_norms, b2_parts, b2_norms)
    own_out[...] = left_sums(labels_of(b2_ref), kernel)
    for_2_out[...] = right_sums(labels_of(own_ref), kernel)


def across_body(
    bm2_ref, b2_ref, b2_parts, b2_norms, for_2_in, for_m2_out, for_2_out, bm2_parts, bm2_norms
):
    split(bm2_ref, bm2_parts, bm2_norms)
    kernel = kernel_tile(bm2_parts, bm2_norms, b2_parts, b2_norms)
    for_m2_out[...] = left_sums(labels_of(b2_ref), kernel)
    for_2_out[...] = for_2_in[...] + right_sums(labels_of(bm2_ref), kernel)


def visitor_body(
    even_ref, own_ref, own_parts, own_norms, bm2_ref, bm2_parts, bm2_norms,
    b2_ref, b2_parts, b2_norms, y_top_ref, y_end_ref,
    own_out, for_m2_out, for_2_out, for_y_out, y_parts, y_norms,
):
    split_pieces(y_top_ref, y_end_ref, y_parts, y_norms)
    y_hot = labels_of(y_top_ref)
    kernel = kernel_tile(own_parts, own_norms, y_parts, y_norms)
    own_out[...] = left_sums(y_hot, kernel)
    for_y_out[...] = right_sums(labels_of(own_ref), kernel)

    @pl.when(even_ref[0] == 1)
    def _():
        kernel = kernel_tile(bm2_parts, bm2_norms, y_parts, y_norms)
        for_m2_out[...] = left_sums(y_hot, kernel)
        for_2_out[...] = jnp.zeros_like(for_2_out)
        for_y_out[...] += right_sums(labels_of(bm2_ref), kernel)

    @pl.when(even_ref[0] == 0)
    def _():
        kernel = kernel_tile(b2_parts, b2_norms, y_parts, y_norms)
        for_2_out[...] = left_sums(y_hot, kernel)
        for_m2_out[...] = jnp.zeros_like(for_m2_out)
        for_y_out[...] += right_sums(labels_of(b2_ref), kernel)


def late_body(
    even_ref, bm2_ref, bm2_parts, bm2_norms, b4_ref, y_top_ref, y_parts, y_norms, for_y_in,
    for_m2_out, for_4_out, for_y_out, b4_parts, b4_norms,
):
    split(b4_ref, b4_parts, b4_norms)
    b4_hot = labels_of(b4_ref)
    kernel = kernel_tile(bm2_parts, bm2_norms, b4_parts, b4_norms)
    for_m2_out[...] = left_sums(b4_hot, kernel)
    for_4_out[...] = right_sums(labels_of(bm2_ref), kernel)
    for_y_out[...] = for_y_in[...]

    @pl.when(even_ref[0] == 0)
    def _():
        kernel = kernel_tile(b4_parts, b4_norms, y_parts, y_norms)
        for_4_out[...] += left_sums(labels_of(y_top_ref), kernel)
        for_y_out[...] += right_sums(b4_hot, kernel)


def choose_body(even_ref, b2_ref, bm2_ref, top_out, end_out):
    cut = top_out.shape[0]

    @pl.when(even_ref[0] == 1)
    def _():
        top_out[...] = b2_ref[:cut, :]
        end_out[...] = b2_ref[cut:, :]

    @pl.when(even_ref[0] == 0)
    def _():
        top_out[...] = bm2_ref[:cut, :]
        end_out[...] = bm2_ref[cut:, :]


def call(body, outs, *args, scratch=(), moved=1000):
    vmem = pl.BlockSpec(memory_space=pltpu.VMEM)
    smem = pl.BlockSpec(memory_space=pltpu.SMEM)
    return pl.pallas_call(
        body,
        out_shape=[pltpu.VMEM(*out) for out in outs],
        in_specs=[smem if a.ndim == 1 else vmem for a in args],
        out_specs=[vmem] * len(outs),
        scratch_shapes=[pltpu.VMEM(*shape) for shape in scratch],
        compiler_params=pltpu.CompilerParams(vmem_limit_bytes=16 * 2**20),
        cost_estimate=pl.CostEstimate(flops=1000, bytes_accessed=moved, transcendentals=0),
    )(*(a if a.ndim == 1 else pltpu.with_memory_space_constraint(a, pltpu.VMEM) for a in args))


def on_device(embeddings, labels):
    even = (1 - lax.axis_index("blk") % 2).astype(jnp.int32)[None]
    own, even = lax.optimization_barrier((pack(embeddings, labels), even))

    b2 = pull(own)
    own_0, *own_split, top, end = call(
        self_body, [SUMS, *SPLIT, *PIECES], own, moved=8 * own.size
    )
    later_own, own_0 = lax.optimization_barrier((own, own_0))
    bm2 = push(later_own)
    sibling = [give(piece, 1) for piece in (top, end)]
    own_0, for_1 = call(
        chip_body, [SUMS] * 2, even, own, *own_split, *sibling, own_0,
        scratch=SPLIT, moved=8 * own.size,
    )
    back_1 = give(for_1, 0)
    b2, own_0, back_1 = lax.optimization_barrier((b2, own_0, back_1))
    b4 = pull(b2)

    own_2, for_2, *b2_split = call(
        near_body, [SUMS] * 2 + [*SPLIT], own, *own_split, b2, moved=8 * own.size
    )
    b2, bm2, for_2 = lax.optimization_barrier((b2, bm2, for_2))
    y_top, y_end = call(choose_body, PIECES, even, b2, bm2, moved=8 * own.size)
    y = swap(y_top), swap(y_end)
    for_m2, for_2, *bm2_split = call(
        across_body, [SUMS] * 2 + [*SPLIT], bm2, b2, *b2_split, for_2, moved=8 * own.size
    )

    y, own_2, for_m2, for_2 = lax.optimization_barrier((y, own_2, for_m2, for_2))
    own_y, for_m2_y, for_2_y, for_y, *y_split = call(
        visitor_body, [SUMS] * 4 + [*SPLIT],
        even, own, *own_split, bm2, *bm2_split, b2, *b2_split, *y, moved=8 * own.size,
    )
    back_m2 = give(for_y, 0)

    b4, own_y, for_m2_y, for_2_y, for_y = lax.optimization_barrier(
        (b4, own_y, for_m2_y, for_2_y, for_y)
    )
    for_m2_4, for_4, for_y = call(
        late_body, [SUMS] * 3, even, bm2, *bm2_split, b4, y[0], *y_split, for_y,
        scratch=SPLIT, moved=16 * own.size,
    )
    back_4 = push(for_4)
    home_m2 = pull(for_m2 + for_m2_y + for_m2_4 + back_m2)
    back_2 = give(for_y, 1)
    back_4, back_2, for_2 = lax.optimization_barrier((back_4, back_2, for_2 + for_2_y))
    home_2 = push(for_2 + back_2 + back_4)
    vmem = pl.BlockSpec(memory_space=pltpu.VMEM)
    parts = own_0, back_1, own_2, own_y, home_m2, home_2
    return pl.pallas_call(
        final_body,
        out_shape=jax.ShapeDtypeStruct((ROWS, CLUSTERS), jnp.float32),
        in_specs=[vmem] * len(parts),
        out_specs=vmem,
        compiler_params=pltpu.CompilerParams(vmem_limit_bytes=16 * 2**20),
    )(*(pltpu.with_memory_space_constraint(part, pltpu.VMEM) for part in parts))


def solution(mesh):
    placed = (P("blk", None), P("blk"))
    return jax.shard_map(
        on_device, mesh=mesh, in_specs=placed, out_specs=P("blk", None), check_vma=False
    )
```
